32 devices in a mesh: groups: 2 (over y), seq: 16 (over z, x, core).
Axes of the slice: x: 2, y: 2, z: 4, core: 2. Of those that a mesh axis runs over, the one named last changes fastest.
Arguments:
- inputs: bfloat16 [4, 8192, 1536], P('groups', 'seq'), parts along dimension 0, may hold values from -6 to 6
- conv_weight: bfloat16 [3, 1536, 768], P(None, 'seq'), may hold values from -0.09375 to 0.09375
- proj_weight: bfloat16 [1536, 768], P('seq'), may hold values from -0.21875 to 0.21875
- cotangent: bfloat16 [4, 8192, 1536], P('groups', 'seq'), parts along dimension 0, may hold values from -6 to 6
Outputs:
- outputs: bfloat16 [4, 8192, 1536], P('groups', 'seq'), parts along dimension 0
- input_grad: bfloat16 [4, 8192, 1536], P('groups', 'seq'), parts along dimension 0
- conv_grad: float32 [3072, 3, 768], P(('groups', 'seq')), parts along dimension 0
- proj_grad: float32 [3072, 768], P(('groups', 'seq')), parts along dimension 0
The draws below stay inside these ranges and needn't reach their ends.
There are 2 independent parts, one for each index of `groups`. The reference program is written for one: setup_inputs(seed, part) draws one part's arguments, and reference() takes and returns one part's arrays. A program takes and returns all parts, laid end to end along the dimension named above; an argument that names none is the same for every part. Nothing has to cross between parts.
All inputs are finite; a program needn't handle non-finite values.
Results may differ from the reference program's by a relative error of at most 0.0051.
Values may be sent and summed in bfloat16 or wider, within the bound.
No kernel may reach another device: no remote copies, remote signals or barrier semaphores. Data moves between devices by JAX's collectives and lax.ppermute only.
A program may use at most 128 MiB of HBM per device.

```python
import jax
import jax.numpy as jnp

C = 1536
H = 768
L = 8192
B = 2


def spiked(array, stream_key, source, target, blocks, factor):
    def block_of(dim):
        return (jnp.arange(array.shape[dim]) // (array.shape[dim] // blocks)).reshape((-1,) + (1,) * (array.ndim - 1 - dim))

    first = jax.random.permutation(stream_key, blocks)[block_of(target)]
    far = (block_of(target) + blocks // 2) % blocks
    return jnp.where((block_of(source) == first) | (block_of(source) == far), factor * array, array)


def block_scale(own_key, shape, pieces, least, high):
    def one(dim, blocks):
        heights = jax.random.uniform(jax.random.fold_in(jax.random.fold_in(own_key, 6), dim), (blocks,), jnp.float32, least / len(pieces), high / len(pieces))
        return jnp.repeat(jnp.exp(heights), shape[dim] // blocks).reshape((-1,) + (1,) * (len(shape) - dim - 1))

    gain = one(*pieces[0])
    for cut in pieces[1:]:
        gain = gain * one(*cut)
    return gain


def normal_values(stream_key, extent, spread, limit, pieces=(), kind=jnp.bfloat16):
    level = block_scale(stream_key, extent, pieces, -0.22, 0.18) if pieces else 1.0
    result = jax.random.normal(stream_key, extent, jnp.float32) * spread * level
    return jnp.minimum(jnp.maximum(result, -limit), limit).astype(kind)


def heavy_noise(rng, extent, deviation, bound, pieces, heavy, dtype=jnp.bfloat16):
    array = deviation * jax.random.normal(rng, extent, jnp.float32)
    if pieces:
        array = array * block_scale(rng, extent, pieces, -0.22, 0.18)
    return jnp.clip(spiked(array, jax.random.fold_in(rng, 3), *heavy), -bound, bound).astype(dtype)


def setup_inputs(seed: int = 0, part: int = 0) -> dict:
    arg_keys = jax.random.split(jax.random.key(seed), 5)
    own_keys = jax.random.split(jax.random.fold_in(arg_keys[4], part), 5)
    return {
        "inputs": heavy_noise(own_keys[0], (B, L, C), 1.0, 6.0, ((1, 16),), (1, 2, 16, 2.0)),
        "conv_weight": normal_values(arg_keys[1], (3, C, H), (3 * C) ** -0.5, 0.09375, ((1, 16),)),
        "proj_weight": normal_values(arg_keys[2], (C, H), H ** -0.5, 0.21875, ((0, 16),)),
        "cotangent": heavy_noise(own_keys[3], (B, L, C), 1.0, 6.0, ((1, 16),), (1, 2, 16, 2.0)),
    }


def shift_rows(values, offset):
    width = values.shape[1]
    if offset > 0:
        padded = jnp.pad(values, ((0, 0), (0, offset), (0, 0)))
        return padded[:, offset:offset + width, :]
    if offset < 0:
        padded = jnp.pad(values, ((0, 0), (-offset, 0), (0, 0)))
        return padded[:, :width, :]
    return values

def gelu_grad(point, upstream):
    return jax.vjp(jax.nn.gelu, point)[1](upstream)[0]

def reference(inputs, conv_weight, proj_weight, cotangent):
    dilation = L // 8
    batch = inputs.shape[0]
    chans = inputs.shape[2]
    hid = conv_weight.shape[2]
    scale = 1.0 / float(batch * L) ** 0.5
    acted = jax.nn.gelu(inputs.astype(jnp.float32)).astype(jnp.bfloat16)
    hidden = jnp.zeros((batch * L, hid), jnp.float32)
    for k in range(3):
        moved = shift_rows(acted, (k - 1) * dilation).reshape(-1, chans)
        hidden = hidden + jnp.dot(moved, conv_weight[k], preferred_element_type=jnp.float32)
    gated = jax.nn.gelu(hidden).astype(jnp.bfloat16)
    outputs = (inputs.reshape(-1, chans).astype(jnp.float32) + jnp.dot(gated, proj_weight.T, preferred_element_type=jnp.float32)).astype(jnp.bfloat16)
    cot_rows = cotangent.reshape(-1, chans)
    gated_grad = jnp.dot(cot_rows, proj_weight, preferred_element_type=jnp.float32)
    hidden_grad = gelu_grad(hidden, gated_grad).astype(jnp.bfloat16)
    grad_blocks = hidden_grad.reshape(batch, L, hid)
    acted_grad = jnp.zeros((batch * L, chans), jnp.float32)
    kernel_parts = []
    for k in range(3):
        moved_grad = shift_rows(grad_blocks, -(k - 1) * dilation).reshape(-1, hid)
        acted_grad = acted_grad + jnp.dot(moved_grad, conv_weight[k].T, preferred_element_type=jnp.float32)
        moved = shift_rows(acted, (k - 1) * dilation).reshape(-1, chans)
        kernel_parts.append(jnp.dot(moved.T, hidden_grad, preferred_element_type=jnp.float32))
    input_grad = (cot_rows.astype(jnp.float32) + gelu_grad(inputs.reshape(-1, chans).astype(jnp.float32), acted_grad)).astype(jnp.bfloat16)
    conv_grad = jnp.stack(kernel_parts, axis=1) * scale
    proj_grad = jnp.dot(cot_rows.T, gated, preferred_element_type=jnp.float32) * scale
    return (outputs.reshape(batch, L, chans), input_grad.reshape(batch, L, chans), conv_grad, proj_grad)
```

```python
import jax
import jax.numpy as jnp
from jax import lax
from jax.sharding import PartitionSpec as P

L = 8192


def from_behind(block, axis, distance):
    devices = range(lax.axis_size(axis))
    route = [(i - distance, i) for i in devices if i - distance in devices]
    return lax.ppermute(block, axis, route)


def gelu_grad(point, upstream):
    return jax.vjp(jax.nn.gelu, point)[1](upstream)[0]


def shards(inputs, conv_weight, proj_weight, cotangent):
    batch, local_len, chans = inputs.shape
    devices = lax.axis_size("seq")
    stride = devices // 8
    scale = 1.0 / float(batch * L) ** 0.5
    acted = jax.nn.gelu(inputs.astype(jnp.float32)).astype(jnp.bfloat16)
    conv_weight, proj_weight = (
        lax.all_gather(conv_weight, "seq", axis=1, tiled=True),
        lax.all_gather(proj_weight, "seq", axis=0, tiled=True),
    )
    hid = conv_weight.shape[2]
    acted_rows = acted.reshape(-1, chans)
    before = from_behind(acted, "seq", stride)
    after = from_behind(acted, "seq", -stride)
    hidden = jnp.dot(before.reshape(-1, chans), conv_weight[0], preferred_element_type=jnp.float32)
    hidden = hidden + jnp.dot(acted_rows, conv_weight[1], preferred_element_type=jnp.float32)
    hidden = hidden + jnp.dot(
        after.reshape(-1, chans), conv_weight[2], preferred_element_type=jnp.float32
    )
    gated = jax.nn.gelu(hidden).astype(jnp.bfloat16)
    outputs = (
        inputs.reshape(-1, chans).astype(jnp.float32)
        + jnp.dot(gated, proj_weight.T, preferred_element_type=jnp.float32)
    ).astype(jnp.bfloat16)
    cot_rows = cotangent.reshape(-1, chans)
    gated_grad = jnp.dot(cot_rows, proj_weight, preferred_element_type=jnp.float32)
    hidden_grad = gelu_grad(hidden, gated_grad).astype(jnp.bfloat16)
    grad_blocks = hidden_grad.reshape(batch, local_len, hid)
    grad_later = from_behind(grad_blocks, "seq", -stride).reshape(-1, hid)
    grad_earlier = from_behind(grad_blocks, "seq", stride).reshape(-1, hid)
    acted_grad = jnp.dot(grad_later, conv_weight[0].T, preferred_element_type=jnp.float32)
    acted_grad = acted_grad + jnp.dot(
        hidden_grad, conv_weight[1].T, preferred_element_type=jnp.float32
    )
    acted_grad = acted_grad + jnp.dot(
        grad_earlier, conv_weight[2].T, preferred_element_type=jnp.float32
    )
    input_grad = (
        cot_rows.astype(jnp.float32)
        + gelu_grad(inputs.reshape(-1, chans).astype(jnp.float32), acted_grad)
    ).astype(jnp.bfloat16)
    tap_grads = (grad_later, hidden_grad, grad_earlier)
    share = chans // devices
    local_terms = [
        jnp.dot(acted_rows.T, piece, preferred_element_type=jnp.float32) for piece in tap_grads
    ]
    local_terms.append(jnp.dot(cot_rows.T, gated, preferred_element_type=jnp.float32))
    stacked = jnp.stack(local_terms, axis=1)
    received = lax.all_to_all(stacked, "seq", split_axis=0, concat_axis=0, tiled=True)
    summed = jnp.sum(received.reshape(devices, share, 4, received.shape[2]), axis=0)
    conv_sum = summed[:, 0:3, :]
    proj_sum = summed[:, 3, :]
    return (
        outputs.reshape(batch, local_len, chans),
        input_grad.reshape(batch, local_len, chans),
        conv_sum * scale,
        proj_sum * scale,
    )


def dot(a, b):
    return jnp.dot(a, b, preferred_element_type=jnp.float32)


def tdot(a, b):
    return lax.dot_general(a, b, (((0,), (0,)), ((), ())), preferred_element_type=jnp.float32)


def dot_t(a, b):
    return lax.dot_general(a, b, (((1,), (1,)), ((), ())), preferred_element_type=jnp.float32)


def paired(inputs, conv_weight, proj_weight, cotangent):
    batch, local_len, chans = inputs.shape
    hid = conv_weight.shape[2]
    devices = lax.axis_size("seq")
    depth = devices // 4
    share = chans // devices
    scale = 1.0 / float(batch * L) ** 0.5
    me = lax.axis_index("seq")
    core, x, z = me % 2, (me // 2) % 2, me // 4
    everyone = range(devices)

    def swap(value, bits):
        return lax.ppermute(value, "seq", [(i, i ^ bits) for i in everyone])

    def up(value):
        return lax.ppermute(value, "seq", [(i, i + 4) for i in everyone if i + 4 in everyone])

    def down(value):
        return lax.ppermute(value, "seq", [(i + 4, i) for i in everyone if i + 4 in everyone])

    def pick(value, index, axis=0):
        return lax.dynamic_index_in_dim(value, index, axis, keepdims=False)

    def exchange(pair):
        kept, got = pick(pair, x), swap(pick(pair, 1 - x), 2)
        first = jnp.where(x == 0, kept, got)
        second = jnp.where(x == 0, got, kept)
        return first, second

    in_a, in_b = exchange(inputs)
    weights = lax.all_gather(
        jnp.concatenate([conv_weight, proj_weight[None]], axis=0), "seq", axis=1, tiled=True
    )
    w0, w1, w2, wp = weights[0], weights[1], weights[2], weights[3]
    cot_a, cot_b = exchange(cotangent)
    cot = jnp.concatenate([cot_a, cot_b], axis=0)

    def act(v):
        return jax.nn.gelu(v.astype(jnp.float32)).astype(jnp.bfloat16)

    act_a, act_b = act(in_a), act(in_b)
    acted = jnp.concatenate([act_a, act_b], axis=0)
    from_prev = up(dot(act_b, w0).astype(jnp.bfloat16))
    from_next = down(dot(act_a, w2).astype(jnp.bfloat16))
    hidden_a = dot(act_a, w1) + dot(act_b, w2) + from_prev.astype(jnp.float32)
    hidden_b = dot(act_b, w1) + dot(act_a, w0) + from_next.astype(jnp.float32)
    hidden = jnp.concatenate([hidden_a, hidden_b], axis=0)
    gated = jax.nn.gelu(hidden).astype(jnp.bfloat16)
    gated_grad = dot(cot, wp)
    hidden_grad = gelu_grad(hidden, gated_grad).astype(jnp.bfloat16)
    hg_a, hg_b = hidden_grad[:local_len], hidden_grad[local_len:]
    hg_prev, hg_next = up(hg_b), down(hg_a)

    def scattered(term):
        cols = term.shape[1]
        parts = term.reshape(depth, 2, 2, share, cols)
        parts = pick(parts, core, 2) + swap(pick(parts, 1 - core, 2), 1)
        parts = pick(parts, x, 1) + swap(pick(parts, 1 - x, 1).astype(jnp.bfloat16), 2).astype(jnp.float32)
        total = pick(parts, z)
        for k in range(1, depth):
            total = total + swap(pick(parts, z ^ k).astype(jnp.bfloat16), 4 * k).astype(jnp.float32)
        return total * scale

    first = scattered(jnp.concatenate([tdot(acted, hidden_grad), tdot(cot, gated)], axis=1))
    gated_own = exchange(gated.reshape(2, local_len, hid))
    gated_own = jnp.concatenate(gated_own, axis=0)
    outputs = (
        inputs.reshape(-1, chans).astype(jnp.float32) + dot_t(gated_own, wp)
    ).astype(jnp.bfloat16)
    left = jnp.concatenate([hg_b, hg_next], axis=0)
    right = jnp.concatenate([hg_prev, hg_a], axis=0)
    second = scattered(tdot(acted, jnp.concatenate([left, right], axis=1)))
    acted_grad = dot_t(left, w0) + dot_t(hidden_grad, w1) + dot_t(right, w2)
    into = jnp.concatenate([in_a, in_b], axis=0).astype(jnp.float32)
    input_grad = (cot.astype(jnp.float32) + gelu_grad(into, acted_grad)).astype(jnp.bfloat16)
    input_grad = jnp.stack(exchange(input_grad.reshape(2, local_len, chans)))
    conv_grad = jnp.stack([second[:, :hid], first[:, :hid], second[:, hid:]], axis=1)
    return (
        outputs.reshape(batch, local_len, chans),
        input_grad,
        conv_grad,
        first[:, hid:],
    )


def solution(mesh):
    def body(inputs, conv_weight, proj_weight, cotangent):
        devices = lax.axis_size("seq")
        by_pairs = devices == 16 and inputs.shape[0] == 2
        return (paired if by_pairs else shards)(inputs, conv_weight, proj_weight, cotangent)

    return jax.shard_map(
        body,
        mesh=mesh,
        in_specs=(
            P("groups", "seq", None),
            P(None, "seq", None),
            P("seq", None),
            P("groups", "seq", None),
        ),
        out_specs=(
            P("groups", "seq", None),
            P("groups", "seq", None),
            P(("groups", "seq"), None, None),
            P(("groups", "seq"), None),
        ),
        check_vma=False,
    )
```

```python
import jax
import jax.numpy as jnp
from jax import lax
from jax.experimental import pallas as pl
from jax.experimental.pallas import tpu as pltpu
from jax.sharding import PartitionSpec as P

L = 8192


def from_behind(block, axis, distance):
    devices = range(lax.axis_size(axis))
    route = [(i - distance, i) for i in devices if i - distance in devices]
    return lax.ppermute(block, axis, route)


def gelu_grad(point, upstream):
    return jax.vjp(jax.nn.gelu, point)[1](upstream)[0]


def shards(inputs, conv_weight, proj_weight, cotangent):
    batch, local_len, chans = inputs.shape
    devices = lax.axis_size("seq")
    stride = devices // 8
    scale = 1.0 / float(batch * L) ** 0.5
    acted = jax.nn.gelu(inputs.astype(jnp.float32)).astype(jnp.bfloat16)
    conv_weight, proj_weight = (
        lax.all_gather(conv_weight, "seq", axis=1, tiled=True),
        lax.all_gather(proj_weight, "seq", axis=0, tiled=True),
    )
    hid = conv_weight.shape[2]
    acted_rows = acted.reshape(-1, chans)
    before = from_behind(acted, "seq", stride)
    after = from_behind(acted, "seq", -stride)
    hidden = jnp.dot(before.reshape(-1, chans), conv_weight[0], preferred_element_type=jnp.float32)
    hidden = hidden + jnp.dot(acted_rows, conv_weight[1], preferred_element_type=jnp.float32)
    hidden = hidden + jnp.dot(
        after.reshape(-1, chans), conv_weight[2], preferred_element_type=jnp.float32
    )
    gated = jax.nn.gelu(hidden).astype(jnp.bfloat16)
    outputs = (
        inputs.reshape(-1, chans).astype(jnp.float32)
        + jnp.dot(gated, proj_weight.T, preferred_element_type=jnp.float32)
    ).astype(jnp.bfloat16)
    cot_rows = cotangent.reshape(-1, chans)
    gated_grad = jnp.dot(cot_rows, proj_weight, preferred_element_type=jnp.float32)
    hidden_grad = gelu_grad(hidden, gated_grad).astype(jnp.bfloat16)
    grad_blocks = hidden_grad.reshape(batch, local_len, hid)
    grad_later = from_behind(grad_blocks, "seq", -stride).reshape(-1, hid)
    grad_earlier = from_behind(grad_blocks, "seq", stride).reshape(-1, hid)
    acted_grad = jnp.dot(grad_later, conv_weight[0].T, preferred_element_type=jnp.float32)
    acted_grad = acted_grad + jnp.dot(
        hidden_grad, conv_weight[1].T, preferred_element_type=jnp.float32
    )
    acted_grad = acted_grad + jnp.dot(
        grad_earlier, conv_weight[2].T, preferred_element_type=jnp.float32
    )
    input_grad = (
        cot_rows.astype(jnp.float32)
        + gelu_grad(inputs.reshape(-1, chans).astype(jnp.float32), acted_grad)
    ).astype(jnp.bfloat16)
    tap_grads = (grad_later, hidden_grad, grad_earlier)
    share = chans // devices
    local_terms = [
        jnp.dot(acted_rows.T, piece, preferred_element_type=jnp.float32) for piece in tap_grads
    ]
    local_terms.append(jnp.dot(cot_rows.T, gated, preferred_element_type=jnp.float32))
    stacked = jnp.stack(local_terms, axis=1)
    received = lax.all_to_all(stacked, "seq", split_axis=0, concat_axis=0, tiled=True)
    summed = jnp.sum(received.reshape(devices, share, 4, received.shape[2]), axis=0)
    conv_sum = summed[:, 0:3, :]
    proj_sum = summed[:, 3, :]
    return (
        outputs.reshape(batch, local_len, chans),
        input_grad.reshape(batch, local_len, chans),
        conv_sum * scale,
        proj_sum * scale,
    )


def dot(a, b):
    return jnp.dot(a, b, preferred_element_type=jnp.float32)


def dot_t(a, b):
    return lax.dot_general(a, b, (((1,), (1,)), ((), ())), preferred_element_type=jnp.float32)


def t_dot(a, b):
    return lax.dot_general(a, b, (((0,), (0,)), ((), ())), preferred_element_type=jnp.float32)


def act(v):
    return jax.nn.gelu(v.astype(jnp.float32)).astype(jnp.bfloat16)


def after(values, *earlier):
    return lax.optimization_barrier((values, earlier))[0]


def call(kernel, outs, place, *args, grid=(), ins=None, out_specs=None, scratch=()):
    whole = pl.BlockSpec(memory_space=pltpu.VMEM)
    ins = [whole] * len(args) if ins is None else ins
    outs = [jax.ShapeDtypeStruct(shape, dtype) for shape, dtype in outs]
    out_specs = [whole] * len(outs) if out_specs is None else out_specs
    light = pl.CostEstimate(flops=1, bytes_accessed=1, transcendentals=0)
    return pl.pallas_call(
        kernel,
        grid=grid,
        out_shape=outs,
        in_specs=[pl.BlockSpec(memory_space=pltpu.SMEM)] + ins,
        out_specs=out_specs,
        scratch_shapes=scratch,
        compiler_params=pltpu.CompilerParams(vmem_limit_bytes=24 * 2**20),
        cost_estimate=light,
    )(place, *args)


def block(shape, *index):
    return pl.BlockSpec(shape, lambda i: tuple(i if d else 0 for d in index))


def place_kernel(place, kept, got, out):
    z, x, core, y = place[0], place[1], place[2], place[3]
    for dy in range(kept.shape[0]):
        for dz in range(kept.shape[1]):
            for dx in range(kept.shape[2]):
                out[z ^ dz, x ^ dx, core, y ^ dy] = kept[dy, dz, dx]
                out[z ^ dz, x ^ dx, 1 - core, y ^ dy] = got[dy, dz, dx]


def placed(place, kept, got):
    ys, depth, xs, rows, cols = kept.shape
    (out,) = call(place_kernel, [((depth, xs, 2, ys, rows, cols), kept.dtype)], place, kept, got)
    return out.reshape(-1, cols)


def tap_kernel(place, rows_sent, rows_kept, tap, sent, kept):
    weight = tap[...]
    sent[...] = dot(rows_sent[...], weight).astype(sent.dtype)
    kept[...] = dot(rows_kept[...], weight)


def gated_kernel(place, near_a, near_b, act_a, act_b, tap, from_prev, from_next, hidden, gated, sent):
    x = place[1]
    weight = tap[...]
    hidden[0] = near_a[...] + dot(act_a[...], weight) + from_prev[...].astype(jnp.float32)
    hidden[1] = near_b[...] + dot(act_b[...], weight) + from_next[...].astype(jnp.float32)
    gated[...] = act(hidden[...])
    sent[...] = gated[1 - x]


def hidden_grad_kernel(place, hidden, cot_a, cot_b, proj, hg_a, hg_b):
    weight = proj[...]
    hg_a[...] = gelu_grad(hidden[0], dot(cot_a[...], weight)).astype(jnp.bfloat16)
    hg_b[...] = gelu_grad(hidden[1], dot(cot_b[...], weight)).astype(jnp.bfloat16)


def term_kernel(place, rows_a, rows_b, grad_a, grad_b, mine, theirs, product):
    core = place[2]
    sums = t_dot(rows_a[...], grad_a[...]) + t_dot(rows_b[...], grad_b[...])
    product[...] = sums.reshape(product.shape)
    mine[:, 0] = product[:, core]
    theirs[:, 0] = product[:, 1 - core].astype(theirs.dtype)


def first_x_kernel(place, mine, got, kept, sent):
    x = place[1]
    kept[...] = mine[x] + got[x].astype(jnp.float32)
    sent[...] = (mine[1 - x] + got[1 - x].astype(jnp.float32)).astype(jnp.bfloat16)


def first_z_kernel(place, mine, got, kept, *sent):
    z = place[0]
    kept[...] = mine[:, z] + got[:, z].astype(jnp.float32)
    for k, out in enumerate(sent, 1):
        out[...] = (mine[:, z ^ k] + got[:, z ^ k].astype(jnp.float32)).astype(jnp.bfloat16)


def then_z_kernel(place, mine, got, kept, *sent):
    z = place[0]
    kept[...] = mine[z] + got[z].astype(jnp.float32)
    for k, out in enumerate(sent, 1):
        out[...] = (mine[z ^ k] + got[z ^ k].astype(jnp.float32)).astype(jnp.bfloat16)


def then_x_kernel(place, mine, *refs):
    x = place[1]
    got, kept, sent = refs[:-2], refs[-2], refs[-1]
    for index, out in ((x, kept), (1 - x, sent)):
        total = mine[index]
        for term in got:
            total = total + term[index].astype(jnp.float32)
        out[...] = total.astype(out.dtype)


def input_grad_kernel(place, hg_next, hg_b, hg_a, hg_prev, w0, w1, w2, in_a, in_b, cot_a, cot_b, kept, sent):
    x = place[1]

    def grad(later, here, earlier, values, cot):
        total = dot_t(later[...], w0[...]) + dot_t(here[...], w1[...]) + dot_t(earlier[...], w2[...])
        wide = values[...].astype(jnp.float32)
        return (cot[...].astype(jnp.float32) + gelu_grad(wide, total)).astype(jnp.bfloat16)

    grad_a = grad(hg_b, hg_a, hg_prev, in_a, cot_a)
    grad_b = grad(hg_next, hg_b, hg_a, in_b, cot_b)

    @pl.when(x == 0)
    def _():
        kept[...] = grad_a
        sent[...] = grad_b

    @pl.when(x != 0)
    def _():
        kept[...] = grad_b
        sent[...] = grad_a


def outputs_kernel(place, gated, got, proj, inputs, outputs):
    x = place[1]
    weight = proj[...]
    for window, rows in ((x, gated[x]), (1 - x, got[...])):
        wide = inputs[window].astype(jnp.float32) + dot_t(rows, weight)
        outputs[window] = wide.astype(jnp.bfloat16)


def paired(inputs, conv_weight, proj_weight, cotangent):
    batch, local_len, chans = inputs.shape
    hid = conv_weight.shape[2]
    devices = lax.axis_size("seq")
    depth = devices // 4
    share = chans // devices
    scale = 1.0 / float(batch * L) ** 0.5
    me, y = lax.axis_index("seq"), lax.axis_index("groups")
    core, x, z = me % 2, (me // 2) % 2, me // 4
    place = jnp.stack([z, x, core, y]).astype(jnp.int32)
    everyone = range(devices)
    bf16, f32 = jnp.bfloat16, jnp.float32
    tile = 256
    steps = chans // tile

    def swap(value, bits):
        return lax.ppermute(value, "seq", [(i, i ^ bits) for i in everyone])

    def up(value):
        return lax.ppermute(value, "seq", [(i, i + 4) for i in everyone if i + 4 in everyone])

    def down(value):
        return lax.ppermute(value, "seq", [(i + 4, i) for i in everyone if i + 4 in everyone])

    def pick(value, index, axis=0):
        return lax.dynamic_index_in_dim(value, index, axis, keepdims=False)

    def ordered(kept, got):
        return jnp.where(x == 0, kept, got), jnp.where(x == 0, got, kept)

    half = share // 2
    shard = jnp.concatenate([conv_weight, proj_weight[None]], axis=0)
    shard = lax.dynamic_slice_in_dim(shard, y * half, half, 1)
    shard_x = swap(shard, 2)
    in_got = swap(after(pick(inputs, 1 - x), shard_x), 2)

    def along_z(k, *earlier):
        piece = after(jnp.stack([shard[k], shard_x[k]]), *earlier)
        return jnp.stack([piece] + [swap(piece, 4 * d) for d in range(1, depth)])

    def over_y(column, *earlier):
        column = after(column, *earlier)
        return jnp.stack([column, lax.ppermute(column, "groups", [(0, 1), (1, 0)])])

    def tap_sums(rows_sent, rows_kept, tap):
        return call(
            tap_kernel,
            [((local_len, hid), bf16), ((local_len, hid), f32)],
            place, rows_sent, rows_kept, tap,
            grid=(hid // tile,),
            ins=[block((local_len, chans), 0, 0)] * 2 + [block((chans, tile), 0, 1)],
            out_specs=[block((local_len, tile), 0, 1)] * 2,
        )

    column_0 = along_z(0)
    column_2 = along_z(2, column_0)
    half_0 = over_y(column_0)
    column_1 = along_z(1, column_2, half_0, in_got)
    half_2 = over_y(column_2, half_0)
    in_a, in_b = ordered(pick(inputs, x), in_got)
    act_a, act_b = act(in_a), act(in_b)
    w0 = placed(place, half_0, swap(half_0, 1))
    to_next, near_b = tap_sums(act_b, act_a, w0)
    from_prev = up(to_next)
    column_p = along_z(3, column_1, half_2, to_next)
    cot_got = swap(after(pick(cotangent, 1 - x), in_got, column_1), 2)
    half_1 = over_y(column_1, half_2)
    w2 = placed(place, half_2, swap(half_2, 1))
    to_prev, near_a = tap_sums(act_a, act_b, after(w2, to_next))
    from_next = down(to_prev)
    half_p = over_y(column_p, half_1, to_prev)
    w1 = placed(place, half_1, swap(after(half_1, from_prev), 1))
    hidden, gated, gated_sent = call(
        gated_kernel,
        [((2, local_len, hid), f32), ((2, local_len, hid), bf16), ((local_len, hid), bf16)],
        place, near_a, near_b, act_a, act_b, after(w1, half_p), from_prev, from_next,
        grid=(hid // tile,),
        ins=[block((local_len, tile), 0, 1)] * 2
        + [block((local_len, chans), 0, 0)] * 2
        + [block((chans, tile), 0, 1)]
        + [block((local_len, tile), 0, 1)] * 2,
        out_specs=[block((2, local_len, tile), 0, 0, 1)] * 2 + [block((local_len, tile), 0, 1)],
    )
    gated_got = swap(gated_sent, 2)
    def term(rows_a, rows_b, grad_a, grad_b):
        cols = 4 * share
        part = (2, depth, share, hid)
        mine, theirs = call(
            term_kernel,
            [(part, f32), (part, bf16)],
            place, rows_a, rows_b, grad_a, grad_b,
            grid=(depth,),
            ins=[block((local_len, cols), 0, 1)] * 2 + [block((local_len, hid), 0, 0)] * 2,
            out_specs=[block((2, 1, share, hid), 0, 1, 0, 0)] * 2,
            scratch=[pltpu.VMEM((2, 2, share, hid), f32)],
        )
        return mine, swap(theirs, 1)

    def x_first(mine, got):
        kept, sent = call(
            first_x_kernel,
            [((depth, share, hid), f32), ((depth, share, hid), bf16)],
            place, mine, got,
            grid=(depth,),
            ins=[block((2, 1, share, hid), 0, 1, 0, 0)] * 2,
            out_specs=[block((1, share, hid), 1, 0, 0)] * 2,
        )
        return kept, swap(sent, 2)

    def then_z(kept, got):
        kept, *sent = call(
            then_z_kernel,
            [((share, hid), f32)] + [((share, hid), bf16)] * (depth - 1),
            place, kept, got,
        )
        return [kept] + [swap(value, 4 * k) for k, value in enumerate(sent, 1)]

    def z_first(mine, got):
        kept, *sent = call(
            first_z_kernel,
            [((2, share, hid), f32)] + [((2, share, hid), bf16)] * (depth - 1),
            place, mine, got,
        )
        return [kept] + [swap(value, 4 * k) for k, value in enumerate(sent, 1)]

    def then_x(kept, *got):
        kept, sent = call(
            then_x_kernel, [((share, hid), f32), ((share, hid), bf16)], place, kept, *got
        )
        return [kept, swap(sent, 2)]

    def total(parts):
        return sum(part.astype(f32) for part in parts)

    cot_a, cot_b = ordered(pick(cotangent, x), cot_got)
    term_p = term(cot_a, cot_b, gated[0], gated[1])
    grad_p = x_first(*term_p)
    wp = placed(place, half_p, swap(after(half_p, from_prev, from_next), 1))
    hg_a, hg_b = call(
        hidden_grad_kernel,
        [((local_len, hid), bf16)] * 2,
        place, hidden, cot_a, cot_b, after(wp, term_p[0]),
        grid=(hid // tile,),
        ins=[block((2, local_len, tile), 0, 0, 1)]
        + [block((local_len, chans), 0, 0)] * 2
        + [block((chans, tile), 0, 1)],
        out_specs=[block((local_len, tile), 0, 1)] * 2,
    )
    hg_prev, hg_next = up(hg_b), down(hg_a)
    grad_p = then_z(after(grad_p[0], hg_prev, hg_next, gated_got), grad_p[1])
    term_1 = term(act_a, act_b, hg_a, after(hg_b, grad_p[0]))
    term_0 = term(act_a, act_b, hg_b, after(hg_next, term_1[0]))
    grad_1 = x_first(after(term_1[0], term_0[0]), term_1[1])
    term_2 = term(act_a, act_b, hg_prev, after(hg_a, grad_1[0]))
    input_kept, input_sent = call(
        input_grad_kernel,
        [((local_len, chans), bf16)] * 2,
        place, hg_next, hg_b, hg_a, after(hg_prev, term_2[0]), w0, w1, w2, in_a, in_b, cot_a, cot_b,
        grid=(steps,),
        ins=[block((local_len, hid), 0, 0)] * 4
        + [block((tile, hid), 1, 0)] * 3
        + [block((local_len, tile), 0, 1)] * 4,
        out_specs=[block((local_len, tile), 0, 1)] * 2,
    )
    grad_0 = x_first(after(term_0[0], input_sent, grad_1[1], grad_p), term_0[1])
    grad_1 = then_z(after(grad_1[0], grad_0[0]), grad_1[1])
    (outputs,) = call(
        outputs_kernel,
        [(inputs.shape, bf16)],
        place, gated, after(gated_got, grad_1[0]), wp, inputs,
        grid=(steps,),
        ins=[
            block((2, local_len, hid), 0, 0, 0),
            block((local_len, hid), 0, 0),
            block((tile, hid), 1, 0),
            block((2, local_len, tile), 0, 0, 1),
        ],
        out_specs=[block((2, local_len, tile), 0, 0, 1)],
    )
    grad_2 = z_first(after(term_2[0], outputs, grad_0[1], grad_1), term_2[1])
    input_got = swap(after(input_sent, grad_0, grad_1), 2)
    grad_2 = then_x(after(grad_2[0], outputs), *grad_2[1:])
    grad_0 = then_z(after(grad_0[0], grad_2[0]), grad_0[1])
    conv_grad = jnp.stack([total(grad_0), total(grad_1), total(grad_2)], axis=1)
    return (
        outputs,
        jnp.stack(ordered(input_kept, input_got)),
        conv_grad * scale,
        total(grad_p) * scale,
    )


def solution(mesh):
    def body(inputs, conv_weight, proj_weight, cotangent):
        devices = lax.axis_size("seq")
        by_pairs = devices == 16 and inputs.shape[0] == 2 and lax.axis_size("groups") == 2
        return (paired if by_pairs else shards)(inputs, conv_weight, proj_weight, cotangent)

    return jax.shard_map(
        body,
        mesh=mesh,
        in_specs=(
            P("groups", "seq", None),
            P(None, "seq", None),
            P("seq", None),
            P("groups", "seq", None),
        ),
        out_specs=(
            P("groups", "seq", None),
            P("groups", "seq", None),
            P(("groups", "seq"), None, None),
            P(("groups", "seq"), None),
        ),
        check_vma=False,
    )
```

```python
import jax
import jax.numpy as jnp
from jax import lax
from jax.experimental import pallas as pl
from jax.experimental.pallas import tpu as pltpu
from jax.sharding import PartitionSpec as P

L = 8192
LONG = 10**10


def from_behind(block, axis, distance):
    devices = range(lax.axis_size(axis))
    route = [(i - distance, i) for i in devices if i - distance in devices]
    return lax.ppermute(block, axis, route)


def gelu_grad(point, upstream):
    return jax.vjp(jax.nn.gelu, point)[1](upstream)[0]


def shards(inputs, conv_weight, proj_weight, cotangent):
    batch, local_len, chans = inputs.shape
    devices = lax.axis_size("seq")
    stride = devices // 8
    scale = 1.0 / float(batch * L) ** 0.5
    acted = jax.nn.gelu(inputs.astype(jnp.float32)).astype(jnp.bfloat16)
    conv_weight, proj_weight = (
        lax.all_gather(conv_weight, "seq", axis=1, tiled=True),
        lax.all_gather(proj_weight, "seq", axis=0, tiled=True),
    )
    hid = conv_weight.shape[2]
    acted_rows = acted.reshape(-1, chans)
    before = from_behind(acted, "seq", stride)
    after = from_behind(acted, "seq", -stride)
    hidden = jnp.dot(before.reshape(-1, chans), conv_weight[0], preferred_element_type=jnp.float32)
    hidden = hidden + jnp.dot(acted_rows, conv_weight[1], preferred_element_type=jnp.float32)
    hidden = hidden + jnp.dot(
        after.reshape(-1, chans), conv_weight[2], preferred_element_type=jnp.float32
    )
    gated = jax.nn.gelu(hidden).astype(jnp.bfloat16)
    outputs = (
        inputs.reshape(-1, chans).astype(jnp.float32)
        + jnp.dot(gated, proj_weight.T, preferred_element_type=jnp.float32)
    ).astype(jnp.bfloat16)
    cot_rows = cotangent.reshape(-1, chans)
    gated_grad = jnp.dot(cot_rows, proj_weight, preferred_element_type=jnp.float32)
    hidden_grad = gelu_grad(hidden, gated_grad).astype(jnp.bfloat16)
    grad_blocks = hidden_grad.reshape(batch, local_len, hid)
    grad_later = from_behind(grad_blocks, "seq", -stride).reshape(-1, hid)
    grad_earlier = from_behind(grad_blocks, "seq", stride).reshape(-1, hid)
    acted_grad = jnp.dot(grad_later, conv_weight[0].T, preferred_element_type=jnp.float32)
    acted_grad = acted_grad + jnp.dot(
        hidden_grad, conv_weight[1].T, preferred_element_type=jnp.float32
    )
    acted_grad = acted_grad + jnp.dot(
        grad_earlier, conv_weight[2].T, preferred_element_type=jnp.float32
    )
    input_grad = (
        cot_rows.astype(jnp.float32)
        + gelu_grad(inputs.reshape(-1, chans).astype(jnp.float32), acted_grad)
    ).astype(jnp.bfloat16)
    tap_grads = (grad_later, hidden_grad, grad_earlier)
    share = chans // devices
    local_terms = [
        jnp.dot(acted_rows.T, piece, preferred_element_type=jnp.float32) for piece in tap_grads
    ]
    local_terms.append(jnp.dot(cot_rows.T, gated, preferred_element_type=jnp.float32))
    stacked = jnp.stack(local_terms, axis=1)
    received = lax.all_to_all(stacked, "seq", split_axis=0, concat_axis=0, tiled=True)
    summed = jnp.sum(received.reshape(devices, share, 4, received.shape[2]), axis=0)
    conv_sum = summed[:, 0:3, :]
    proj_sum = summed[:, 3, :]
    return (
        outputs.reshape(batch, local_len, chans),
        input_grad.reshape(batch, local_len, chans),
        conv_sum * scale,
        proj_sum * scale,
    )


def dot(a, b):
    return jnp.dot(a, b, preferred_element_type=jnp.float32)


def dot_t(a, b):
    return lax.dot_general(a, b, (((1,), (1,)), ((), ())), preferred_element_type=jnp.float32)


def t_dot(a, b):
    return lax.dot_general(a, b, (((0,), (0,)), ((), ())), preferred_element_type=jnp.float32)


def act(v):
    return jax.nn.gelu(v.astype(jnp.float32)).astype(jnp.bfloat16)


def after(values, *earlier):
    return lax.optimization_barrier((values, earlier))[0]


def call(kernel, outs, place, *args, grid=(), ins=None, out_specs=None, scratch=(), work=1):
    whole = pl.BlockSpec(memory_space=pltpu.VMEM)
    ins = [whole] * len(args) if ins is None else ins
    outs = [jax.ShapeDtypeStruct(shape, dtype) for shape, dtype in outs]
    out_specs = [whole] * len(outs) if out_specs is None else out_specs
    light = pl.CostEstimate(flops=work, bytes_accessed=1, transcendentals=0)
    return pl.pallas_call(
        kernel,
        grid=grid,
        out_shape=outs,
        in_specs=[pl.BlockSpec(memory_space=pltpu.SMEM)] + ins,
        out_specs=out_specs,
        scratch_shapes=scratch,
        compiler_params=pltpu.CompilerParams(vmem_limit_bytes=24 * 2**20),
        cost_estimate=light,
    )(place, *args)


def block(shape, *index):
    return pl.BlockSpec(shape, lambda i: tuple(i if d else 0 for d in index))


def place_kernel(place, kept, got, out):
    z, x, core, y = place[0], place[1], place[2], place[3]
    for dy in range(kept.shape[0]):
        for dz in range(kept.shape[1]):
            for dx in range(kept.shape[2]):
                out[z ^ dz, x ^ dx, core, y ^ dy] = kept[dy, dz, dx]
                out[z ^ dz, x ^ dx, 1 - core, y ^ dy] = got[dy, dz, dx]


def placed(place, kept, got):
    ys, depth, xs, rows, cols = kept.shape
    (out,) = call(place_kernel, [((depth, xs, 2, ys, rows, cols), kept.dtype)], place, kept, got)
    return out.reshape(-1, cols)


def tap_kernel(place, rows_sent, rows_kept, tap, sent, kept):
    weight = tap[...]
    sent[...] = dot(rows_sent[...], weight).astype(sent.dtype)
    kept[...] = dot(rows_kept[...], weight)


def own_tap_kernel(place, near_a, near_b, act_a, act_b, tap, sum_a, sum_b):
    weight = tap[...]
    sum_a[...] = near_a[...] + dot(act_a[...], weight)
    sum_b[...] = near_b[...] + dot(act_b[...], weight)


def gated_kernel(place, near_a, near_b, from_prev, from_next, hidden, gated, sent):
    x = place[1]
    hidden[0] = near_a[...] + from_prev[...].astype(jnp.float32)
    hidden[1] = near_b[...] + from_next[...].astype(jnp.float32)
    gated[...] = act(hidden[...])
    sent[...] = gated[1 - x]


def hidden_grad_kernel(place, hidden, cot_a, cot_b, proj, hg_a, hg_b):
    weight = proj[...]
    hg_a[...] = gelu_grad(hidden[0], dot(cot_a[...], weight)).astype(jnp.bfloat16)
    hg_b[...] = gelu_grad(hidden[1], dot(cot_b[...], weight)).astype(jnp.bfloat16)


def term_kernel(place, rows_a, rows_b, grad_a, grad_b, mine, theirs, product):
    core = place[2]
    sums = t_dot(rows_a[...], grad_a[...]) + t_dot(rows_b[...], grad_b[...])
    product[...] = sums.reshape(product.shape)
    mine[:, 0] = product[:, core]
    theirs[:, 0] = product[:, 1 - core].astype(theirs.dtype)


def first_x_kernel(place, mine, got, kept, sent):
    x = place[1]
    kept[...] = mine[x] + got[x].astype(jnp.float32)
    sent[...] = (mine[1 - x] + got[1 - x].astype(jnp.float32)).astype(jnp.bfloat16)


def then_z_kernel(place, mine, got, kept, *sent):
    z = place[0]
    kept[...] = mine[z] + got[z].astype(jnp.float32)
    for k, out in enumerate(sent, 1):
        out[...] = (mine[z ^ k] + got[z ^ k].astype(jnp.float32)).astype(jnp.bfloat16)


def input_grad_kernel(place, hg_next, hg_b, hg_a, hg_prev, w0, w1, w2, in_a, in_b, cot_a, cot_b, kept, sent):
    x = place[1]

    def grad(later, here, earlier, values, cot):
        total = dot_t(later[...], w0[...]) + dot_t(here[...], w1[...]) + dot_t(earlier[...], w2[...])
        wide = values[...].astype(jnp.float32)
        return (cot[...].astype(jnp.float32) + gelu_grad(wide, total)).astype(jnp.bfloat16)

    grad_a = grad(hg_b, hg_a, hg_prev, in_a, cot_a)
    grad_b = grad(hg_next, hg_b, hg_a, in_b, cot_b)

    @pl.when(x == 0)
    def _():
        kept[...] = grad_a
        sent[...] = grad_b

    @pl.when(x != 0)
    def _():
        kept[...] = grad_b
        sent[...] = grad_a


def outputs_kernel(place, gated, got, proj, inputs, outputs):
    x = place[1]
    weight = proj[...]
    for window, rows in ((x, gated[x]), (1 - x, got[...])):
        wide = inputs[window].astype(jnp.float32) + dot_t(rows, weight)
        outputs[window] = wide.astype(jnp.bfloat16)


def paired(inputs, conv_weight, proj_weight, cotangent):
    batch, local_len, chans = inputs.shape
    hid = conv_weight.shape[2]
    devices = lax.axis_size("seq")
    depth = devices // 4
    share = chans // devices
    scale = 1.0 / float(batch * L) ** 0.5
    me, y = lax.axis_index("seq"), lax.axis_index("groups")
    core, x, z = me % 2, (me // 2) % 2, me // 4
    place = jnp.stack([z, x, core, y]).astype(jnp.int32)
    everyone = range(devices)
    bf16, f32 = jnp.bfloat16, jnp.float32
    tile = 256
    steps = chans // tile

    def swap(value, bits):
        return lax.ppermute(value, "seq", [(i, i ^ bits) for i in everyone])

    def up(value):
        return lax.ppermute(value, "seq", [(i, i + 4) for i in everyone if i + 4 in everyone])

    def down(value):
        return lax.ppermute(value, "seq", [(i + 4, i) for i in everyone if i + 4 in everyone])

    def pick(value, index, axis=0):
        return lax.dynamic_index_in_dim(value, index, axis, keepdims=False)

    def ordered(kept, got):
        return jnp.where(x == 0, kept, got), jnp.where(x == 0, got, kept)

    half = share // 2
    shard = jnp.concatenate([conv_weight, proj_weight[None]], axis=0)
    shard = lax.dynamic_slice_in_dim(shard, y * half, half, 1)
    shard_x = swap(shard, 2)
    in_got = swap(after(pick(inputs, 1 - x), shard_x), 2)

    def along_z(k, *earlier):
        piece = after(jnp.stack([shard[k], shard_x[k]]), *earlier)
        return jnp.stack([piece] + [swap(piece, 4 * d) for d in range(1, depth)])

    def over_y(column, *earlier):
        column = after(column, *earlier)
        return jnp.stack([column, lax.ppermute(column, "groups", [(0, 1), (1, 0)])])

    def tap_sums(rows_sent, rows_kept, tap):
        return call(
            tap_kernel,
            [((local_len, hid), bf16), ((local_len, hid), f32)],
            place, rows_sent, rows_kept, tap,
            grid=(hid // tile,),
            ins=[block((local_len, chans), 0, 0)] * 2 + [block((chans, tile), 0, 1)],
            out_specs=[block((local_len, tile), 0, 1)] * 2,
        )

    column_0 = along_z(0)
    column_2 = along_z(2, column_0)
    half_0 = over_y(column_0)
    in_a, in_b = ordered(pick(inputs, x), in_got)
    act_a, act_b = act(in_a), act(in_b)
    column_1 = along_z(1, column_2, half_0, act_a, act_b)
    half_2 = over_y(column_2, half_0)
    w0 = placed(place, half_0, swap(half_0, 1))
    to_next, near_b = tap_sums(act_b, act_a, w0)
    from_prev = up(to_next)
    cot_got = swap(after(pick(cotangent, 1 - x), in_got, column_1), 2)
    half_1 = over_y(column_1, half_2)
    piece_p = after(jnp.stack([shard[3], shard_x[3]]), column_1, half_2, to_next)
    column_p = [swap(piece_p, 12), swap(piece_p, 8)]
    w2 = placed(place, half_2, swap(after(half_2, to_next), 1))
    column_p = jnp.stack([piece_p, swap(after(piece_p, w2), 4)] + column_p[::-1])
    to_prev, near_a = tap_sums(act_a, act_b, after(w2, to_next))
    from_next = down(to_prev)
    half_p = over_y(column_p, half_1, to_prev)
    w1 = placed(place, half_1, swap(half_1, 1))
    near_a, near_b = call(
        own_tap_kernel,
        [((local_len, hid), f32)] * 2,
        place, near_a, near_b, act_a, act_b, w1,
        grid=(hid // tile,),
        ins=[block((local_len, tile), 0, 1)] * 2
        + [block((local_len, chans), 0, 0)] * 2
        + [block((chans, tile), 0, 1)],
        out_specs=[block((local_len, tile), 0, 1)] * 2,
    )
    hidden, gated, gated_sent = call(
        gated_kernel,
        [((2, local_len, hid), f32), ((2, local_len, hid), bf16), ((local_len, hid), bf16)],
        place, near_a, near_b, from_prev, after(from_next, near_a),
        grid=(hid // tile,),
        ins=[block((local_len, tile), 0, 1)] * 4,
        out_specs=[block((2, local_len, tile), 0, 0, 1)] * 2 + [block((local_len, tile), 0, 1)],
    )
    gated_got = swap(gated_sent, 2)
    def term(rows_a, rows_b, grad_a, grad_b, work=1):
        cols = 4 * share
        part = (2, depth, share, hid)
        mine, theirs = call(
            term_kernel,
            [(part, f32), (part, bf16)],
            place, rows_a, rows_b, grad_a, grad_b,
            grid=(depth,),
            ins=[block((local_len, cols), 0, 1)] * 2 + [block((local_len, hid), 0, 0)] * 2,
            out_specs=[block((2, 1, share, hid), 0, 1, 0, 0)] * 2,
            scratch=[pltpu.VMEM((2, 2, share, hid), f32)],
            work=work,
        )
        return mine, swap(theirs, 1)

    def x_first(mine, got):
        kept, sent = call(
            first_x_kernel,
            [((depth, share, hid), f32), ((depth, share, hid), bf16)],
            place, mine, got,
            grid=(depth,),
            ins=[block((2, 1, share, hid), 0, 1, 0, 0)] * 2,
            out_specs=[block((1, share, hid), 1, 0, 0)] * 2,
        )
        return kept, swap(sent, 2)

    def then_z(kept, got):
        kept, *sent = call(
            then_z_kernel,
            [((share, hid), f32)] + [((share, hid), bf16)] * (depth - 1),
            place, kept, got,
        )
        return [kept] + [swap(value, 4 * k) for k, value in enumerate(sent, 1)]

    def total(parts):
        return sum(part.astype(f32) for part in parts)

    cot_a, cot_b = ordered(pick(cotangent, x), cot_got)
    term_p = term(cot_a, cot_b, gated[0], gated[1])
    wp = placed(place, half_p, swap(after(half_p, from_prev, from_next, near_a, near_b), 1))
    hg_a, hg_b = call(
        hidden_grad_kernel,
        [((local_len, hid), bf16)] * 2,
        place, hidden, cot_a, cot_b, after(wp, term_p[0]),
        grid=(hid // tile,),
        ins=[block((2, local_len, tile), 0, 0, 1)]
        + [block((local_len, chans), 0, 0)] * 2
        + [block((chans, tile), 0, 1)],
        out_specs=[block((local_len, tile), 0, 1)] * 2,
        work=LONG,
    )
    hg_prev, hg_next = up(hg_b), down(hg_a)
    grad_p = x_first(after(term_p[0], hg_a, gated_got), term_p[1])
    term_1 = term(act_a, act_b, hg_a, after(hg_b, grad_p[0]))
    term_0 = term(act_a, act_b, hg_b, after(hg_next, term_1[0], hg_prev), LONG)
    grad_1 = x_first(after(term_1[0], term_0[0], grad_p[1]), term_1[1])
    term_2 = term(act_a, act_b, hg_prev, after(hg_a, grad_1[0]))
    grad_p = then_z(after(grad_p[0], term_2[0]), grad_p[1])

    def input_grads(part, *earlier):
        cols = [block((local_len, tile), 0, 1)]
        first = part * steps // 2
        late = pl.BlockSpec((local_len, tile), lambda i: (0, i + first))
        taps = pl.BlockSpec((tile, hid), lambda i: (i + first, 0))
        return call(
            input_grad_kernel,
            [((local_len, chans // 2), bf16)] * 2,
            place, hg_next, hg_b, hg_a, after(hg_prev, *earlier), w0, w1, w2, in_a, in_b, cot_a, cot_b,
            grid=(steps // 2,),
            ins=[block((local_len, hid), 0, 0)] * 4 + [taps] * 3 + [late] * 4,
            out_specs=cols * 2,
        )

    grad_0 = x_first(after(term_0[0], grad_p[0]), term_0[1])
    kept_0, sent_0 = input_grads(0, grad_0[0])
    grad_1 = then_z(after(grad_1[0], sent_0, grad_p), grad_1[1])
    grad_2 = x_first(after(term_2[0], grad_1[0]), term_2[1])
    kept_1, sent_1 = input_grads(1, grad_2[0])
    (outputs,) = call(
        outputs_kernel,
        [(inputs.shape, bf16)],
        place, gated, after(gated_got, sent_1), wp, inputs,
        grid=(steps,),
        ins=[
            block((2, local_len, hid), 0, 0, 0),
            block((local_len, hid), 0, 0),
            block((tile, hid), 1, 0),
            block((2, local_len, tile), 0, 0, 1),
        ],
        out_specs=[block((2, local_len, tile), 0, 0, 1)],
    )
    grad_0 = then_z(after(grad_0[0], outputs, grad_1), grad_0[1])
    got_0 = swap(after(sent_0, grad_0[0]), 2)
    grad_2 = then_z(after(grad_2[0], grad_0), grad_2[1])
    got_1 = swap(after(sent_1, grad_2[0]), 2)
    input_kept = jnp.concatenate([kept_0, kept_1], axis=1)
    input_got = jnp.concatenate([got_0, got_1], axis=1)
    conv_grad = jnp.stack([total(grad_0), total(grad_1), total(grad_2)], axis=1)
    return (
        outputs,
        jnp.stack(ordered(input_kept, input_got)),
        conv_grad * scale,
        total(grad_p) * scale,
    )


def solution(mesh):
    def body(inputs, conv_weight, proj_weight, cotangent):
        devices = lax.axis_size("seq")
        by_pairs = devices == 16 and inputs.shape[0] == 2 and lax.axis_size("groups") == 2
        return (paired if by_pairs else shards)(inputs, conv_weight, proj_weight, cotangent)

    return jax.shard_map(
        body,
        mesh=mesh,
        in_specs=(
            P("groups", "seq", None),
            P(None, "seq", None),
            P("seq", None),
            P("groups", "seq", None),
        ),
        out_specs=(
            P("groups", "seq", None),
            P("groups", "seq", None),
            P(("groups", "seq"), None, None),
            P(("groups", "seq"), None),
        ),
        check_vma=False,
    )
```

```python
import jax
import jax.numpy as jnp
from jax import lax
from jax.experimental import pallas as pl
from jax.experimental.pallas import tpu as pltpu
from jax.sharding import PartitionSpec as P

L = 8192
LONG = 10**10


def from_behind(block, axis, distance):
    devices = range(lax.axis_size(axis))
    route = [(i - distance, i) for i in devices if i - distance in devices]
    return lax.ppermute(block, axis, route)


def gelu_grad(point, upstream):
    return jax.vjp(jax.nn.gelu, point)[1](upstream)[0]


def shards(inputs, conv_weight, proj_weight, cotangent):
    batch, local_len, chans = inputs.shape
    devices = lax.axis_size("seq")
    stride = devices // 8
    scale = 1.0 / float(batch * L) ** 0.5
    acted = jax.nn.gelu(inputs.astype(jnp.float32)).astype(jnp.bfloat16)
    conv_weight, proj_weight = (
        lax.all_gather(conv_weight, "seq", axis=1, tiled=True),
        lax.all_gather(proj_weight, "seq", axis=0, tiled=True),
    )
    hid = conv_weight.shape[2]
    acted_rows = acted.reshape(-1, chans)
    before = from_behind(acted, "seq", stride)
    after = from_behind(acted, "seq", -stride)
    hidden = jnp.dot(before.reshape(-1, chans), conv_weight[0], preferred_element_type=jnp.float32)
    hidden = hidden + jnp.dot(acted_rows, conv_weight[1], preferred_element_type=jnp.float32)
    hidden = hidden + jnp.dot(
        after.reshape(-1, chans), conv_weight[2], preferred_element_type=jnp.float32
    )
    gated = jax.nn.gelu(hidden).astype(jnp.bfloat16)
    outputs = (
        inputs.reshape(-1, chans).astype(jnp.float32)
        + jnp.dot(gated, proj_weight.T, preferred_element_type=jnp.float32)
    ).astype(jnp.bfloat16)
    cot_rows = cotangent.reshape(-1, chans)
    gated_grad = jnp.dot(cot_rows, proj_weight, preferred_element_type=jnp.float32)
    hidden_grad = gelu_grad(hidden, gated_grad).astype(jnp.bfloat16)
    grad_blocks = hidden_grad.reshape(batch, local_len, hid)
    grad_later = from_behind(grad_blocks, "seq", -stride).reshape(-1, hid)
    grad_earlier = from_behind(grad_blocks, "seq", stride).reshape(-1, hid)
    acted_grad = jnp.dot(grad_later, conv_weight[0].T, preferred_element_type=jnp.float32)
    acted_grad = acted_grad + jnp.dot(
        hidden_grad, conv_weight[1].T, preferred_element_type=jnp.float32
    )
    acted_grad = acted_grad + jnp.dot(
        grad_earlier, conv_weight[2].T, preferred_element_type=jnp.float32
    )
    input_grad = (
        cot_rows.astype(jnp.float32)
        + gelu_grad(inputs.reshape(-1, chans).astype(jnp.float32), acted_grad)
    ).astype(jnp.bfloat16)
    tap_grads = (grad_later, hidden_grad, grad_earlier)
    share = chans // devices
    local_terms = [
        jnp.dot(acted_rows.T, piece, preferred_element_type=jnp.float32) for piece in tap_grads
    ]
    local_terms.append(jnp.dot(cot_rows.T, gated, preferred_element_type=jnp.float32))
    stacked = jnp.stack(local_terms, axis=1)
    received = lax.all_to_all(stacked, "seq", split_axis=0, concat_axis=0, tiled=True)
    summed = jnp.sum(received.reshape(devices, share, 4, received.shape[2]), axis=0)
    conv_sum = summed[:, 0:3, :]
    proj_sum = summed[:, 3, :]
    return (
        outputs.reshape(batch, local_len, chans),
        input_grad.reshape(batch, local_len, chans),
        conv_sum * scale,
        proj_sum * scale,
    )


def dot(a, b):
    return jnp.dot(a, b, preferred_element_type=jnp.float32)


def dot_t(a, b):
    return lax.dot_general(a, b, (((1,), (1,)), ((), ())), preferred_element_type=jnp.float32)


def t_dot(a, b):
    return lax.dot_general(a, b, (((0,), (0,)), ((), ())), preferred_element_type=jnp.float32)


def act(v):
    return jax.nn.gelu(v.astype(jnp.float32)).astype(jnp.bfloat16)


def after(values, *earlier):
    return lax.optimization_barrier((values, earlier))[0]


def call(kernel, outs, place, *args, grid=(), ins=None, out_specs=None, scratch=(), work=1):
    whole = pl.BlockSpec(memory_space=pltpu.VMEM)
    ins = [whole] * len(args) if ins is None else ins
    outs = [jax.ShapeDtypeStruct(shape, dtype) for shape, dtype in outs]
    out_specs = [whole] * len(outs) if out_specs is None else out_specs
    light = pl.CostEstimate(flops=work, bytes_accessed=1, transcendentals=0)
    return pl.pallas_call(
        kernel,
        grid=grid,
        out_shape=outs,
        in_specs=[pl.BlockSpec(memory_space=pltpu.SMEM)] + ins,
        out_specs=out_specs,
        scratch_shapes=scratch,
        compiler_params=pltpu.CompilerParams(vmem_limit_bytes=24 * 2**20),
        cost_estimate=light,
    )(place, *args)


def block(shape, *index):
    return pl.BlockSpec(shape, lambda i: tuple(i if d else 0 for d in index))


RESIDENT = pl.BlockSpec(memory_space=pltpu.VMEM)


def place_kernel(place, kept, got, out):
    z, x, core, y = place[0], place[1], place[2], place[3]
    for dy in range(kept.shape[0]):
        for dz in range(kept.shape[1]):
            for dx in range(kept.shape[2]):
                out[z ^ dz, x ^ dx, core, y ^ dy] = kept[dy, dz, dx]
                out[z ^ dz, x ^ dx, 1 - core, y ^ dy] = got[dy, dz, dx]


def placed(place, kept, got):
    ys, depth, xs, rows, cols = kept.shape
    (out,) = call(place_kernel, [((depth, xs, 2, ys, rows, cols), kept.dtype)], place, kept, got)
    return out.reshape(-1, cols)


def tap_kernel(place, rows_sent, rows_kept, tap, sent, kept):
    weight = tap[...]
    sent[...] = dot(rows_sent[...], weight).astype(sent.dtype)
    kept[...] = dot(rows_kept[...], weight)


def own_tap_kernel(place, near_a, near_b, act_a, act_b, tap, sum_a, sum_b):
    weight = tap[...]
    sum_a[...] = near_a[...] + dot(act_a[...], weight)
    sum_b[...] = near_b[...] + dot(act_b[...], weight)


def gated_kernel(place, near_a, near_b, from_prev, from_next, hidden, gated, sent):
    x = place[1]
    hidden[0] = near_a[...] + from_prev[...].astype(jnp.float32)
    hidden[1] = near_b[...] + from_next[...].astype(jnp.float32)
    gated[...] = act(hidden[...])
    sent[...] = gated[1 - x]


def hidden_grad_kernel(place, hidden, cot_a, cot_b, proj, hg_a, hg_b):
    weight = proj[...]
    hg_a[...] = gelu_grad(hidden[0], dot(cot_a[...], weight)).astype(jnp.bfloat16)
    hg_b[...] = gelu_grad(hidden[1], dot(cot_b[...], weight)).astype(jnp.bfloat16)


def term_kernel(place, rows_a, rows_b, grad_a, grad_b, mine, theirs, product):
    core = place[2]
    sums = t_dot(rows_a[...], grad_a[...]) + t_dot(rows_b[...], grad_b[...])
    product[...] = sums.reshape(product.shape)
    mine[:, 0] = product[:, core]
    theirs[:, 0] = product[:, 1 - core].astype(theirs.dtype)


def turn_kernel(place, rows_a, rows_b, out):
    half = rows_a.shape[0]
    out[:, :half] = rows_a[...].T
    out[:, half:] = rows_b[...].T


def turned_term_kernel(place, turned, grad_a, grad_b, mine, theirs, product):
    core = place[2]
    half = grad_a.shape[0]
    sums = dot(turned[:, :half], grad_a[...]) + dot(turned[:, half:], grad_b[...])
    product[...] = sums.reshape(product.shape)
    mine[:, 0] = product[:, core]
    theirs[:, 0] = product[:, 1 - core].astype(theirs.dtype)


def first_x_kernel(place, mine, got, kept, sent):
    x = place[1]
    kept[...] = mine[x] + got[x].astype(jnp.float32)
    sent[...] = (mine[1 - x] + got[1 - x].astype(jnp.float32)).astype(jnp.bfloat16)


def then_z_kernel(place, mine, got, kept, *sent):
    z = place[0]
    kept[...] = mine[z] + got[z].astype(jnp.float32)
    for k, out in enumerate(sent, 1):
        out[...] = (mine[z ^ k] + got[z ^ k].astype(jnp.float32)).astype(jnp.bfloat16)


def input_grad_kernel(place, hg_next, hg_b, hg_a, hg_prev, w0, w1, w2, in_a, in_b, cot_a, cot_b, kept, sent):
    x = place[1]

    def grad(later, here, earlier, values, cot):
        total = dot_t(later[...], w0[...]) + dot_t(here[...], w1[...]) + dot_t(earlier[...], w2[...])
        wide = values[...].astype(jnp.float32)
        return (cot[...].astype(jnp.float32) + gelu_grad(wide, total)).astype(jnp.bfloat16)

    grad_a = grad(hg_b, hg_a, hg_prev, in_a, cot_a)
    grad_b = grad(hg_next, hg_b, hg_a, in_b, cot_b)

    @pl.when(x == 0)
    def _():
        kept[...] = grad_a
        sent[...] = grad_b

    @pl.when(x != 0)
    def _():
        kept[...] = grad_b
        sent[...] = grad_a


def outputs_kernel(place, gated, got, proj, inputs, outputs):
    x = place[1]
    weight = proj[...]
    for window, rows in ((x, gated[x]), (1 - x, got[...])):
        wide = inputs[window].astype(jnp.float32) + dot_t(rows, weight)
        outputs[window] = wide.astype(jnp.bfloat16)


def paired(inputs, conv_weight, proj_weight, cotangent):
    batch, local_len, chans = inputs.shape
    hid = conv_weight.shape[2]
    devices = lax.axis_size("seq")
    depth = devices // 4
    share = chans // devices
    scale = 1.0 / float(batch * L) ** 0.5
    me, y = lax.axis_index("seq"), lax.axis_index("groups")
    core, x, z = me % 2, (me // 2) % 2, me // 4
    place = jnp.stack([z, x, core, y]).astype(jnp.int32)
    everyone = range(devices)
    bf16, f32 = jnp.bfloat16, jnp.float32
    tile = 256
    steps = chans // tile

    def swap(value, bits):
        return lax.ppermute(value, "seq", [(i, i ^ bits) for i in everyone])

    def up(value):
        return lax.ppermute(value, "seq", [(i, i + 4) for i in everyone if i + 4 in everyone])

    def down(value):
        return lax.ppermute(value, "seq", [(i + 4, i) for i in everyone if i + 4 in everyone])

    def pick(value, index, axis=0):
        return lax.dynamic_index_in_dim(value, index, axis, keepdims=False)

    def ordered(kept, got):
        return jnp.where(x == 0, kept, got), jnp.where(x == 0, got, kept)

    half = share // 2
    shard = jnp.concatenate([conv_weight, proj_weight[None]], axis=0)
    shard = lax.dynamic_slice_in_dim(shard, y * half, half, 1)
    shard_x = swap(shard, 2)
    in_got = swap(after(pick(inputs, 1 - x), shard_x), 2)

    def along_z(piece):
        return jnp.stack([piece] + [swap(piece, 4 * d) for d in range(1, depth)])

    def column(k):
        return jnp.stack([shard[k], shard_x[k]])

    def over_y(column):
        return jnp.stack([column, lax.ppermute(column, "groups", [(0, 1), (1, 0)])])

    def tap_sums(rows_sent, rows_kept, tap):
        return call(
            tap_kernel,
            [((local_len, hid), bf16), ((local_len, hid), f32)],
            place, rows_sent, rows_kept, tap,
            grid=(hid // tile,),
            ins=[RESIDENT] * 2 + [block((chans, tile), 0, 1)],
            out_specs=[block((local_len, tile), 0, 1)] * 2,
        )

    column_0 = along_z(column(0))
    column_2 = along_z(after(column(2), column_0))
    half_0 = over_y(column_0)
    in_a, in_b = ordered(pick(inputs, x), in_got)
    act_a, act_b = act(in_a), act(in_b)
    column_1 = along_z(after(column(1), column_2, half_0, (act_a, act_b)))
    half_2 = over_y(after(column_2, half_0))
    w0 = placed(place, half_0, swap(half_0, 1))
    cot_got = swap(after(pick(cotangent, 1 - x), in_got, column_1), 2)
    to_next, near_b = tap_sums(act_b, act_a, w0)
    from_prev = up(to_next)
    w2 = placed(place, half_2, swap(after(half_2, to_next), 1))
    half_1 = over_y(after(column_1, half_2))
    to_prev, near_a = tap_sums(act_a, act_b, after(w2, to_next))
    from_next = down(to_prev)
    piece_p = after(column(3), column_1, half_2, to_next)
    column_p = [swap(piece_p, 12), swap(piece_p, 8)]
    column_p = jnp.stack([piece_p, swap(after(piece_p, w2), 4)] + column_p[::-1])
    half_p = over_y(after(column_p, half_1, to_prev))
    w1 = placed(place, half_1, swap(half_1, 1))
    near_a, near_b = call(
        own_tap_kernel,
        [((local_len, hid), f32)] * 2,
        place, near_a, near_b, act_a, act_b, w1,
        grid=(hid // tile,),
        ins=[block((local_len, tile), 0, 1)] * 2
        + [RESIDENT] * 2
        + [block((chans, tile), 0, 1)],
        out_specs=[block((local_len, tile), 0, 1)] * 2,
        work=1,
    )
    hidden, gated, gated_sent = call(
        gated_kernel,
        [((2, local_len, hid), f32), ((2, local_len, hid), bf16), ((local_len, hid), bf16)],
        place, near_a, near_b, from_prev, after(from_next, near_a),
        grid=(hid // tile,),
        ins=[block((local_len, tile), 0, 1)] * 4,
        out_specs=[block((2, local_len, tile), 0, 0, 1)] * 2 + [block((local_len, tile), 0, 1)],
    )
    gated_got = swap(gated_sent, 2)

    def turned(rows_a, rows_b):
        cols = 4 * share
        return call(
            turn_kernel,
            [((chans, 2 * local_len), bf16)],
            place, rows_a, rows_b,
            grid=(depth,),
            ins=[block((local_len, cols), 0, 1)] * 2,
            out_specs=[block((cols, 2 * local_len), 1, 0)],
        )[0]

    def term(lhs, grad_a, grad_b, work=1):
        cols = 4 * share
        part = (2, depth, share, hid)
        one = len(lhs) == 1
        mine, theirs = call(
            turned_term_kernel if one else term_kernel,
            [(part, f32), (part, bf16)],
            place, *lhs, grad_a, grad_b,
            grid=(depth,),
            ins=([block((cols, 2 * local_len), 1, 0)] if one else [block((local_len, cols), 0, 1)] * 2) + [RESIDENT] * 2,
            out_specs=[block((2, 1, share, hid), 0, 1, 0, 0)] * 2,
            scratch=[pltpu.VMEM((2, 2, share, hid), f32)],
            work=work,
        )
        return mine, swap(theirs, 1)

    def x_first(mine, got):
        kept, sent = call(
            first_x_kernel,
            [((depth, share, hid), f32), ((depth, share, hid), bf16)],
            place, mine, got,
            grid=(depth,),
            ins=[block((2, 1, share, hid), 0, 1, 0, 0)] * 2,
            out_specs=[block((1, share, hid), 1, 0, 0)] * 2,
        )
        return kept, swap(sent, 2)

    def then_z(kept, got):
        kept, *sent = call(
            then_z_kernel,
            [((share, hid), f32)] + [((share, hid), bf16)] * (depth - 1),
            place, kept, got,
        )
        return [kept] + [swap(value, 4 * k) for k, value in enumerate(sent, 1)]

    def total(parts):
        return sum(part.astype(f32) for part in parts)

    cot_a, cot_b = ordered(pick(cotangent, x), cot_got)
    wp = placed(place, half_p, swap(after(half_p, from_prev, from_next, (near_a, near_b)), 1))
    term_p = term((cot_a, cot_b), gated[0], gated[1], 1)
    hg_a, hg_b = call(
        hidden_grad_kernel,
        [((local_len, hid), bf16)] * 2,
        place, hidden, cot_a, cot_b, after(wp, term_p[0]),
        grid=(hid // tile,),
        ins=[block((2, local_len, tile), 0, 0, 1)]
        + [RESIDENT] * 2
        + [block((chans, tile), 0, 1)],
        out_specs=[block((local_len, tile), 0, 1)] * 2,
        work=LONG,
    )
    hg_prev, hg_next = up(hg_b), down(hg_a)

    def input_grads(part, earlier):
        cols = [block((local_len, tile), 0, 1)]
        first = part * steps // 2
        late = pl.BlockSpec((local_len, tile), lambda i: (0, i + first))
        taps = pl.BlockSpec((tile, hid), lambda i: (i + first, 0))
        return call(
            input_grad_kernel,
            [((local_len, chans // 2), bf16)] * 2,
            place, hg_next, hg_b, hg_a, after(hg_prev, earlier), w0, w1, w2, in_a, in_b, cot_a, cot_b,
            grid=(steps // 2,),
            ins=[RESIDENT] * 4 + [taps] * 3 + [late] * 4,
            out_specs=cols * 2,
        )

    grad_p = x_first(after(term_p[0], hg_a, gated_got), term_p[1])
    acted = (turned(act_a, after(act_b, grad_p[0])),)
    term_1 = term(acted, hg_a, after(hg_b, grad_p[0]), 1)

    def finished(got):
        return call(
            outputs_kernel,
            [(inputs.shape, bf16)],
            place, gated, got, wp, inputs,
            grid=(steps,),
            ins=[
                block((2, local_len, hid), 0, 0, 0),
                block((local_len, hid), 0, 0),
                block((tile, hid), 1, 0),
                block((2, local_len, tile), 0, 0, 1),
            ],
            out_specs=[block((2, local_len, tile), 0, 0, 1)],
        )[0]

    term_0 = term(acted, hg_b, after(hg_next, term_1[0], hg_prev), LONG)
    grad_1 = x_first(after(term_1[0], term_0[0], grad_p[1]), term_1[1])
    term_2 = term(acted, hg_prev, after(hg_a, grad_1[0]), 1)
    grad_p = then_z(after(grad_p[0], term_2[0]), grad_p[1])
    grad_0 = x_first(after(term_0[0], grad_p[0]), term_0[1])
    kept_0, sent_0 = input_grads(0, grad_0[0])
    grad_1 = then_z(after(grad_1[0], sent_0, grad_p), grad_1[1])
    grad_2 = x_first(after(term_2[0], grad_1[0]), term_2[1])
    kept_1, sent_1 = input_grads(1, grad_2[0])
    got_0 = swap(sent_0, 2)
    grad_0 = then_z(after(grad_0[0], sent_1, grad_1), grad_0[1])
    outputs = finished(after(gated_got, got_0))
    grad_2 = then_z(after(grad_2[0], grad_0[0], grad_0, outputs), grad_2[1])
    got_1 = swap(after(sent_1, grad_2[0]), 2)
    input_kept = jnp.concatenate([kept_0, kept_1], axis=1)
    input_got = jnp.concatenate([got_0, got_1], axis=1)
    input_grad = jnp.stack(ordered(input_kept, input_got))
    conv_grad = jnp.stack([total(grad_0), total(grad_1), total(grad_2)], axis=1)
    return (
        outputs,
        input_grad,
        conv_grad * scale,
        total(grad_p) * scale,
    )


def solution(mesh):
    def body(inputs, conv_weight, proj_weight, cotangent):
        devices = lax.axis_size("seq")
        by_pairs = devices == 16 and inputs.shape[0] == 2 and lax.axis_size("groups") == 2
        return (paired if by_pairs else shards)(inputs, conv_weight, proj_weight, cotangent)

    return jax.shard_map(
        body,
        mesh=mesh,
        in_specs=(
            P("groups", "seq", None),
            P(None, "seq", None),
            P("seq", None),
            P("groups", "seq", None),
        ),
        out_specs=(
            P("groups", "seq", None),
            P("groups", "seq", None),
            P(("groups", "seq"), None, None),
            P(("groups", "seq"), None),
        ),
        check_vma=False,
    )
```

```python
import jax
import jax.numpy as jnp
from jax import lax
from jax.experimental import pallas as pl
from jax.experimental.pallas import tpu as pltpu
from jax.sharding import PartitionSpec as P

L = 8192
LONG = 10**10


def from_behind(block, axis, distance):
    devices = range(lax.axis_size(axis))
    route = [(i - distance, i) for i in devices if i - distance in devices]
    return lax.ppermute(block, axis, route)


def gelu_grad(point, upstream):
    return jax.vjp(jax.nn.gelu, point)[1](upstream)[0]


def shards(inputs, conv_weight, proj_weight, cotangent):
    batch, local_len, chans = inputs.shape
    devices = lax.axis_size("seq")
    stride = devices // 8
    scale = 1.0 / float(batch * L) ** 0.5
    acted = jax.nn.gelu(inputs.astype(jnp.float32)).astype(jnp.bfloat16)
    conv_weight, proj_weight = (
        lax.all_gather(conv_weight, "seq", axis=1, tiled=True),
        lax.all_gather(proj_weight, "seq", axis=0, tiled=True),
    )
    hid = conv_weight.shape[2]
    acted_rows = acted.reshape(-1, chans)
    before = from_behind(acted, "seq", stride)
    after = from_behind(acted, "seq", -stride)
    hidden = jnp.dot(before.reshape(-1, chans), conv_weight[0], preferred_element_type=jnp.float32)
    hidden = hidden + jnp.dot(acted_rows, conv_weight[1], preferred_element_type=jnp.float32)
    hidden = hidden + jnp.dot(
        after.reshape(-1, chans), conv_weight[2], preferred_element_type=jnp.float32
    )
    gated = jax.nn.gelu(hidden).astype(jnp.bfloat16)
    outputs = (
        inputs.reshape(-1, chans).astype(jnp.float32)
        + jnp.dot(gated, proj_weight.T, preferred_element_type=jnp.float32)
    ).astype(jnp.bfloat16)
    cot_rows = cotangent.reshape(-1, chans)
    gated_grad = jnp.dot(cot_rows, proj_weight, preferred_element_type=jnp.float32)
    hidden_grad = gelu_grad(hidden, gated_grad).astype(jnp.bfloat16)
    grad_blocks = hidden_grad.reshape(batch, local_len, hid)
    grad_later = from_behind(grad_blocks, "seq", -stride).reshape(-1, hid)
    grad_earlier = from_behind(grad_blocks, "seq", stride).reshape(-1, hid)
    acted_grad = jnp.dot(grad_later, conv_weight[0].T, preferred_element_type=jnp.float32)
    acted_grad = acted_grad + jnp.dot(
        hidden_grad, conv_weight[1].T, preferred_element_type=jnp.float32
    )
    acted_grad = acted_grad + jnp.dot(
        grad_earlier, conv_weight[2].T, preferred_element_type=jnp.float32
    )
    input_grad = (
        cot_rows.astype(jnp.float32)
        + gelu_grad(inputs.reshape(-1, chans).astype(jnp.float32), acted_grad)
    ).astype(jnp.bfloat16)
    tap_grads = (grad_later, hidden_grad, grad_earlier)
    share = chans // devices
    local_terms = [
        jnp.dot(acted_rows.T, piece, preferred_element_type=jnp.float32) for piece in tap_grads
    ]
    local_terms.append(jnp.dot(cot_rows.T, gated, preferred_element_type=jnp.float32))
    stacked = jnp.stack(local_terms, axis=1)
    received = lax.all_to_all(stacked, "seq", split_axis=0, concat_axis=0, tiled=True)
    summed = jnp.sum(received.reshape(devices, share, 4, received.shape[2]), axis=0)
    conv_sum = summed[:, 0:3, :]
    proj_sum = summed[:, 3, :]
    return (
        outputs.reshape(batch, local_len, chans),
        input_grad.reshape(batch, local_len, chans),
        conv_sum * scale,
        proj_sum * scale,
    )


def dot(a, b):
    return jnp.dot(a, b, preferred_element_type=jnp.float32)


def dot_t(a, b):
    return lax.dot_general(a, b, (((1,), (1,)), ((), ())), preferred_element_type=jnp.float32)


def t_dot(a, b):
    return lax.dot_general(a, b, (((0,), (0,)), ((), ())), preferred_element_type=jnp.float32)


def act(v):
    return jax.nn.gelu(v.astype(jnp.float32)).astype(jnp.bfloat16)


def after(values, *earlier):
    return lax.optimization_barrier((values, earlier))[0]


def call(kernel, outs, place, *args, grid=(), ins=None, out_specs=None, scratch=(), work=1):
    whole = pl.BlockSpec(memory_space=pltpu.VMEM)
    ins = [whole] * len(args) if ins is None else ins
    outs = [jax.ShapeDtypeStruct(shape, dtype) for shape, dtype in outs]
    out_specs = [whole] * len(outs) if out_specs is None else out_specs
    light = pl.CostEstimate(flops=work, bytes_accessed=1, transcendentals=0)
    return pl.pallas_call(
        kernel,
        grid=grid,
        out_shape=outs,
        in_specs=[pl.BlockSpec(memory_space=pltpu.SMEM)] + ins,
        out_specs=out_specs,
        scratch_shapes=scratch,
        compiler_params=pltpu.CompilerParams(vmem_limit_bytes=24 * 2**20),
        cost_estimate=light,
    )(place, *args)


def block(shape, *index):
    return pl.BlockSpec(shape, lambda i: tuple(i if d else 0 for d in index))


RESIDENT = pl.BlockSpec(memory_space=pltpu.VMEM)


def place_kernel(place, kept, got, out):
    z, x, core, y = place[0], place[1], place[2], place[3]
    for dy in range(kept.shape[0]):
        for dz in range(kept.shape[1]):
            for dx in range(kept.shape[2]):
                out[z ^ dz, x ^ dx, core, y ^ dy] = kept[dy, dz, dx]
                out[z ^ dz, x ^ dx, 1 - core, y ^ dy] = got[dy, dz, dx]


def placed(place, kept, got):
    ys, depth, xs, rows, cols = kept.shape
    (out,) = call(place_kernel, [((depth, xs, 2, ys, rows, cols), kept.dtype)], place, kept, got)
    return out.reshape(-1, cols)


def tap_kernel(place, rows_sent, rows_kept, tap, sent, kept):
    weight = tap[...]
    sent[...] = dot(rows_sent[...], weight).astype(sent.dtype)
    kept[...] = dot(rows_kept[...], weight)


def own_tap_kernel(place, near_a, near_b, act_a, act_b, tap, sum_a, sum_b):
    weight = tap[...]
    sum_a[...] = near_a[...] + dot(act_a[...], weight)
    sum_b[...] = near_b[...] + dot(act_b[...], weight)


def gated_kernel(place, near_a, near_b, from_prev, from_next, hidden, gated, sent):
    x = place[1]
    hidden[0] = near_a[...] + from_prev[...].astype(jnp.float32)
    hidden[1] = near_b[...] + from_next[...].astype(jnp.float32)
    gated[...] = act(hidden[...])
    sent[...] = gated[1 - x]


def hidden_grad_kernel(place, hidden, cot_a, cot_b, proj, hg_a, hg_b):
    weight = proj[...]
    hg_a[...] = gelu_grad(hidden[0], dot(cot_a[...], weight)).astype(jnp.bfloat16)
    hg_b[...] = gelu_grad(hidden[1], dot(cot_b[...], weight)).astype(jnp.bfloat16)


def term_kernel(place, rows_a, rows_b, grad_a, grad_b, mine, theirs, product):
    core = place[2]
    sums = t_dot(rows_a[...], grad_a[...]) + t_dot(rows_b[...], grad_b[...])
    product[...] = sums.reshape(product.shape)
    mine[:, 0] = product[:, core]
    theirs[:, 0] = product[:, 1 - core].astype(theirs.dtype)


def turn_kernel(place, rows_a, rows_b, out):
    half = rows_a.shape[0]
    out[:, :half] = rows_a[...].T
    out[:, half:] = rows_b[...].T


def turned_term_kernel(place, turned, grad_a, grad_b, mine, theirs, product):
    core = place[2]
    half = grad_a.shape[0]
    sums = dot(turned[:, :half], grad_a[...]) + dot(turned[:, half:], grad_b[...])
    product[...] = sums.reshape(product.shape)
    mine[:, 0] = product[:, core]
    theirs[:, 0] = product[:, 1 - core].astype(theirs.dtype)


def first_x_kernel(place, mine, got, kept, sent):
    x = place[1]
    kept[...] = mine[x] + got[x].astype(jnp.float32)
    sent[...] = (mine[1 - x] + got[1 - x].astype(jnp.float32)).astype(jnp.bfloat16)


def then_z_kernel(place, mine, got, kept, *sent):
    z = place[0]
    kept[...] = mine[z] + got[z].astype(jnp.float32)
    for k, out in enumerate(sent, 1):
        out[...] = (mine[z ^ k] + got[z ^ k].astype(jnp.float32)).astype(jnp.bfloat16)


def input_grad_kernel(place, hg_next, hg_b, hg_a, hg_prev, w0, w1, w2, in_a, in_b, cot_a, cot_b, kept, sent):
    x = place[1]

    def grad(later, here, earlier, values, cot):
        total = dot_t(later[...], w0[...]) + dot_t(here[...], w1[...]) + dot_t(earlier[...], w2[...])
        wide = values[...].astype(jnp.float32)
        return (cot[...].astype(jnp.float32) + gelu_grad(wide, total)).astype(jnp.bfloat16)

    grad_a = grad(hg_b, hg_a, hg_prev, in_a, cot_a)
    grad_b = grad(hg_next, hg_b, hg_a, in_b, cot_b)

    @pl.when(x == 0)
    def _():
        kept[...] = grad_a
        sent[...] = grad_b

    @pl.when(x != 0)
    def _():
        kept[...] = grad_b
        sent[...] = grad_a


def outputs_kernel(place, gated, got, proj, inputs, outputs):
    x = place[1]
    weight = proj[...]
    for window, rows in ((x, gated[x]), (1 - x, got[...])):
        wide = inputs[window].astype(jnp.float32) + dot_t(rows, weight)
        outputs[window] = wide.astype(jnp.bfloat16)


def paired(inputs, conv_weight, proj_weight, cotangent):
    batch, local_len, chans = inputs.shape
    hid = conv_weight.shape[2]
    devices = lax.axis_size("seq")
    depth = devices // 4
    share = chans // devices
    scale = 1.0 / float(batch * L) ** 0.5
    me, y = lax.axis_index("seq"), lax.axis_index("groups")
    core, x, z = me % 2, (me // 2) % 2, me // 4
    place = jnp.stack([z, x, core, y]).astype(jnp.int32)
    everyone = range(devices)
    bf16, f32 = jnp.bfloat16, jnp.float32
    tile = 256
    steps = chans // tile

    def swap(value, bits):
        return lax.ppermute(value, "seq", [(i, i ^ bits) for i in everyone])

    def up(value):
        return lax.ppermute(value, "seq", [(i, i + 4) for i in everyone if i + 4 in everyone])

    def down(value):
        return lax.ppermute(value, "seq", [(i + 4, i) for i in everyone if i + 4 in everyone])

    def pick(value, index, axis=0):
        return lax.dynamic_index_in_dim(value, index, axis, keepdims=False)

    def ordered(kept, got):
        return jnp.where(x == 0, kept, got), jnp.where(x == 0, got, kept)

    half = share // 2
    shard = jnp.concatenate([conv_weight, proj_weight[None]], axis=0)
    shard = lax.dynamic_slice_in_dim(shard, y * half, half, 1)
    shard_x = swap(shard, 2)
    in_got = swap(after(pick(inputs, 1 - x), shard_x), 2)

    def along_z(piece):
        return jnp.stack([piece] + [swap(piece, 4 * d) for d in range(1, depth)])

    def column(k):
        return jnp.stack([shard[k], shard_x[k]])

    def over_y(column):
        return jnp.stack([column, lax.ppermute(column, "groups", [(0, 1), (1, 0)])])

    def tap_sums(rows_sent, rows_kept, tap):
        return call(
            tap_kernel,
            [((local_len, hid), bf16), ((local_len, hid), f32)],
            place, rows_sent, rows_kept, tap,
            grid=(hid // tile,),
            ins=[RESIDENT] * 2 + [block((chans, tile), 0, 1)],
            out_specs=[block((local_len, tile), 0, 1)] * 2,
        )

    column_0 = along_z(column(0))
    column_2 = along_z(after(column(2), column_0))
    half_0 = over_y(column_0)
    in_a, in_b = ordered(pick(inputs, x), in_got)
    act_a, act_b = act(in_a), act(in_b)
    column_1 = along_z(after(column(1), column_2, half_0))
    half_2 = over_y(after(column_2, half_0))
    w0 = placed(place, half_0, swap(half_0, 1))
    cot_got = swap(after(pick(cotangent, 1 - x), in_got, column_1), 2)
    to_next, near_b = tap_sums(act_b, act_a, w0)
    from_prev = up(to_next)
    w2 = placed(place, half_2, swap(after(half_2, to_next, column_1), 1))
    half_1 = over_y(after(column_1, half_2))
    to_prev, near_a = tap_sums(act_a, act_b, after(w2, to_next))
    from_next = down(to_prev)
    piece_p = after(column(3), column_1, half_2, to_next)
    column_p = [swap(piece_p, 12), swap(piece_p, 8)]
    column_p = jnp.stack([piece_p, swap(after(piece_p, w2), 4)] + column_p[::-1])
    half_p = over_y(after(column_p, half_1, to_prev))
    w1 = placed(place, half_1, swap(half_1, 1))
    near_a, near_b = call(
        own_tap_kernel,
        [((local_len, hid), f32)] * 2,
        place, near_a, near_b, act_a, act_b, w1,
        grid=(hid // tile,),
        ins=[block((local_len, tile), 0, 1)] * 2
        + [RESIDENT] * 2
        + [block((chans, tile), 0, 1)],
        out_specs=[block((local_len, tile), 0, 1)] * 2,
        work=1,
    )
    hidden, gated, gated_sent = call(
        gated_kernel,
        [((2, local_len, hid), f32), ((2, local_len, hid), bf16), ((local_len, hid), bf16)],
        place, near_a, near_b, from_prev, from_next,
        grid=(hid // tile,),
        ins=[block((local_len, tile), 0, 1)] * 4,
        out_specs=[block((2, local_len, tile), 0, 0, 1)] * 2 + [block((local_len, tile), 0, 1)],
    )
    gated_got = swap(gated_sent, 2)

    def turned(rows_a, rows_b):
        cols = 4 * share
        return call(
            turn_kernel,
            [((chans, 2 * local_len), bf16)],
            place, rows_a, rows_b,
            grid=(depth,),
            ins=[block((local_len, cols), 0, 1)] * 2,
            out_specs=[block((cols, 2 * local_len), 1, 0)],
        )[0]

    def term(lhs, grad_a, grad_b, work=1):
        cols = 4 * share
        part = (2, depth, share, hid)
        one = len(lhs) == 1
        mine, theirs = call(
            turned_term_kernel if one else term_kernel,
            [(part, f32), (part, bf16)],
            place, *lhs, grad_a, grad_b,
            grid=(depth,),
            ins=([block((cols, 2 * local_len), 1, 0)] if one else [block((local_len, cols), 0, 1)] * 2) + [RESIDENT] * 2,
            out_specs=[block((2, 1, share, hid), 0, 1, 0, 0)] * 2,
            scratch=[pltpu.VMEM((2, 2, share, hid), f32)],
            work=work,
        )
        return mine, swap(theirs, 1)

    def x_first(mine, got):
        kept, sent = call(
            first_x_kernel,
            [((depth, share, hid), f32), ((depth, share, hid), bf16)],
            place, mine, got,
            grid=(depth,),
            ins=[block((2, 1, share, hid), 0, 1, 0, 0)] * 2,
            out_specs=[block((1, share, hid), 1, 0, 0)] * 2,
        )
        return kept, swap(sent, 2)

    def then_z(kept, got):
        kept, *sent = call(
            then_z_kernel,
            [((share, hid), f32)] + [((share, hid), bf16)] * (depth - 1),
            place, kept, got,
        )
        return [kept] + [swap(value, 4 * k) for k, value in enumerate(sent, 1)]

    def total(parts):
        return sum(part.astype(f32) for part in parts)

    cot_a, cot_b = ordered(pick(cotangent, x), cot_got)
    wp = placed(place, half_p, swap(after(half_p, from_prev, from_next, (near_a, near_b), (cot_a, cot_b)), 1))
    term_p = term((cot_a, cot_b), gated[0], gated[1], 1)
    hg_a, hg_b = call(
        hidden_grad_kernel,
        [((local_len, hid), bf16)] * 2,
        place, hidden, cot_a, cot_b, after(wp, term_p[0]),
        grid=(hid // tile,),
        ins=[block((2, local_len, tile), 0, 0, 1)]
        + [RESIDENT] * 2
        + [block((chans, tile), 0, 1)],
        out_specs=[block((local_len, tile), 0, 1)] * 2,
        work=LONG,
    )
    hg_prev, hg_next = up(hg_b), down(hg_a)

    def input_grads(part, earlier):
        cols = [block((local_len, tile), 0, 1)]
        first = part * steps // 2
        late = pl.BlockSpec((local_len, tile), lambda i: (0, i + first))
        taps = pl.BlockSpec((tile, hid), lambda i: (i + first, 0))
        return call(
            input_grad_kernel,
            [((local_len, chans // 2), bf16)] * 2,
            place, hg_next, hg_b, hg_a, after(hg_prev, earlier), w0, w1, w2, in_a, in_b, cot_a, cot_b,
            grid=(steps // 2,),
            ins=[RESIDENT] * 4 + [taps] * 3 + [late] * 4,
            out_specs=cols * 2,
        )

    grad_p = x_first(after(term_p[0], hg_a, gated_got), term_p[1])
    acted = (turned(act_a, after(act_b, grad_p[0])),)
    term_1 = term(acted, hg_a, after(hg_b, grad_p[0]), 1)

    def finished(got):
        return call(
            outputs_kernel,
            [(inputs.shape, bf16)],
            place, gated, got, wp, inputs,
            grid=(steps,),
            ins=[
                block((2, local_len, hid), 0, 0, 0),
                block((local_len, hid), 0, 0),
                block((tile, hid), 1, 0),
                block((2, local_len, tile), 0, 0, 1),
            ],
            out_specs=[block((2, local_len, tile), 0, 0, 1)],
        )[0]

    term_0 = term(acted, hg_b, after(hg_next, term_1[0], hg_prev), LONG)
    grad_1 = x_first(after(term_1[0], term_0[0], grad_p[1]), term_1[1])
    term_2 = term(acted, hg_prev, after(hg_a, grad_1[0]), 1)
    grad_p = then_z(after(grad_p[0], grad_1[0], term_2[0]), grad_p[1])
    grad_0 = x_first(after(term_0[0], grad_p[0]), term_0[1])
    kept_0, sent_0 = input_grads(0, grad_0[0])
    grad_1 = then_z(after(grad_1[0], sent_0, grad_p), grad_1[1])
    grad_2 = x_first(after(term_2[0], grad_1[0]), term_2[1])
    kept_1, sent_1 = input_grads(1, grad_2[0])
    got_0 = swap(sent_0, 2)
    grad_0 = then_z(after(grad_0[0], sent_1, grad_1), grad_0[1])
    outputs = finished(after(gated_got, got_0))
    grad_2 = then_z(after(grad_2[0], grad_0[0], grad_0, outputs), grad_2[1])
    got_1 = swap(after(sent_1, grad_2[0]), 2)
    input_kept = jnp.concatenate([kept_0, kept_1], axis=1)
    input_got = jnp.concatenate([got_0, got_1], axis=1)
    input_grad = jnp.stack(ordered(input_kept, input_got))
    conv_grad = jnp.stack([total(grad_0), total(grad_1), total(grad_2)], axis=1)
    return (
        outputs,
        input_grad,
        conv_grad * scale,
        total(grad_p) * scale,
    )


def solution(mesh):
    def body(inputs, conv_weight, proj_weight, cotangent):
        devices = lax.axis_size("seq")
        by_pairs = devices == 16 and inputs.shape[0] == 2 and lax.axis_size("groups") == 2
        return (paired if by_pairs else shards)(inputs, conv_weight, proj_weight, cotangent)

    return jax.shard_map(
        body,
        mesh=mesh,
        in_specs=(
            P("groups", "seq", None),
            P(None, "seq", None),
            P("seq", None),
            P("groups", "seq", None),
        ),
        out_specs=(
            P("groups", "seq", None),
            P("groups", "seq", None),
            P(("groups", "seq"), None, None),
            P(("groups", "seq"), None),
        ),
        check_vma=False,
    )
```

```python
import jax
import jax.numpy as jnp
from jax import lax
from jax.experimental import pallas as pl
from jax.experimental.pallas import tpu as pltpu
from jax.sharding import PartitionSpec as P

L = 8192
LONG = 10**10


def from_behind(block, axis, distance):
    devices = range(lax.axis_size(axis))
    route = [(i - distance, i) for i in devices if i - distance in devices]
    return lax.ppermute(block, axis, route)


def gelu_grad(point, upstream):
    return jax.vjp(jax.nn.gelu, point)[1](upstream)[0]


def shards(inputs, conv_weight, proj_weight, cotangent):
    batch, local_len, chans = inputs.shape
    devices = lax.axis_size("seq")
    stride = devices // 8
    scale = 1.0 / float(batch * L) ** 0.5
    acted = jax.nn.gelu(inputs.astype(jnp.float32)).astype(jnp.bfloat16)
    conv_weight, proj_weight = (
        lax.all_gather(conv_weight, "seq", axis=1, tiled=True),
        lax.all_gather(proj_weight, "seq", axis=0, tiled=True),
    )
    hid = conv_weight.shape[2]
    acted_rows = acted.reshape(-1, chans)
    before = from_behind(acted, "seq", stride)
    after = from_behind(acted, "seq", -stride)
    hidden = jnp.dot(before.reshape(-1, chans), conv_weight[0], preferred_element_type=jnp.float32)
    hidden = hidden + jnp.dot(acted_rows, conv_weight[1], preferred_element_type=jnp.float32)
    hidden = hidden + jnp.dot(
        after.reshape(-1, chans), conv_weight[2], preferred_element_type=jnp.float32
    )
    gated = jax.nn.gelu(hidden).astype(jnp.bfloat16)
    outputs = (
        inputs.reshape(-1, chans).astype(jnp.float32)
        + jnp.dot(gated, proj_weight.T, preferred_element_type=jnp.float32)
    ).astype(jnp.bfloat16)
    cot_rows = cotangent.reshape(-1, chans)
    gated_grad = jnp.dot(cot_rows, proj_weight, preferred_element_type=jnp.float32)
    hidden_grad = gelu_grad(hidden, gated_grad).astype(jnp.bfloat16)
    grad_blocks = hidden_grad.reshape(batch, local_len, hid)
    grad_later = from_behind(grad_blocks, "seq", -stride).reshape(-1, hid)
    grad_earlier = from_behind(grad_blocks, "seq", stride).reshape(-1, hid)
    acted_grad = jnp.dot(grad_later, conv_weight[0].T, preferred_element_type=jnp.float32)
    acted_grad = acted_grad + jnp.dot(
        hidden_grad, conv_weight[1].T, preferred_element_type=jnp.float32
    )
    acted_grad = acted_grad + jnp.dot(
        grad_earlier, conv_weight[2].T, preferred_element_type=jnp.float32
    )
    input_grad = (
        cot_rows.astype(jnp.float32)
        + gelu_grad(inputs.reshape(-1, chans).astype(jnp.float32), acted_grad)
    ).astype(jnp.bfloat16)
    tap_grads = (grad_later, hidden_grad, grad_earlier)
    share = chans // devices
    local_terms = [
        jnp.dot(acted_rows.T, piece, preferred_element_type=jnp.float32) for piece in tap_grads
    ]
    local_terms.append(jnp.dot(cot_rows.T, gated, preferred_element_type=jnp.float32))
    stacked = jnp.stack(local_terms, axis=1)
    received = lax.all_to_all(stacked, "seq", split_axis=0, concat_axis=0, tiled=True)
    summed = jnp.sum(received.reshape(devices, share, 4, received.shape[2]), axis=0)
    conv_sum = summed[:, 0:3, :]
    proj_sum = summed[:, 3, :]
    return (
        outputs.reshape(batch, local_len, chans),
        input_grad.reshape(batch, local_len, chans),
        conv_sum * scale,
        proj_sum * scale,
    )


def dot(a, b):
    return jnp.dot(a, b, preferred_element_type=jnp.float32)


def dot_t(a, b):
    return lax.dot_general(a, b, (((1,), (1,)), ((), ())), preferred_element_type=jnp.float32)


def t_dot(a, b):
    return lax.dot_general(a, b, (((0,), (0,)), ((), ())), preferred_element_type=jnp.float32)


def act(v):
    return jax.nn.gelu(v.astype(jnp.float32)).astype(jnp.bfloat16)


def after(values, *earlier):
    return lax.optimization_barrier((values, earlier))[0]


def call(kernel, outs, place, *args, grid=(), ins=None, out_specs=None, scratch=(), work=1):
    whole = pl.BlockSpec(memory_space=pltpu.VMEM)
    ins = [whole] * len(args) if ins is None else ins
    outs = [jax.ShapeDtypeStruct(shape, dtype) for shape, dtype in outs]
    out_specs = [whole] * len(outs) if out_specs is None else out_specs
    light = pl.CostEstimate(flops=work, bytes_accessed=1, transcendentals=0)
    return pl.pallas_call(
        kernel,
        grid=grid,
        out_shape=outs,
        in_specs=[pl.BlockSpec(memory_space=pltpu.SMEM)] + ins,
        out_specs=out_specs,
        scratch_shapes=scratch,
        compiler_params=pltpu.CompilerParams(vmem_limit_bytes=24 * 2**20),
        cost_estimate=light,
    )(place, *args)


def block(shape, *index):
    return pl.BlockSpec(shape, lambda i: tuple(i if d else 0 for d in index))


RESIDENT = pl.BlockSpec(memory_space=pltpu.VMEM)


def place_kernel(place, kept, got, out):
    z, x, core, y = place[0], place[1], place[2], place[3]
    for dy in range(kept.shape[0]):
        for dz in range(kept.shape[1]):
            for dx in range(kept.shape[2]):
                out[z ^ dz, x ^ dx, core, y ^ dy] = kept[dy, dz, dx]
                out[z ^ dz, x ^ dx, 1 - core, y ^ dy] = got[dy, dz, dx]


def placed(place, kept, got):
    ys, depth, xs, rows, cols = kept.shape
    (out,) = call(place_kernel, [((depth, xs, 2, ys, rows, cols), kept.dtype)], place, kept, got)
    return out.reshape(-1, cols)


def tap_kernel(place, rows_sent, rows_kept, tap, sent, kept):
    weight = tap[...]
    sent[...] = dot(rows_sent[...], weight).astype(sent.dtype)
    kept[...] = dot(rows_kept[...], weight)


def own_tap_kernel(place, near_a, near_b, act_a, act_b, tap, sum_a, sum_b):
    weight = tap[...]
    sum_a[...] = near_a[...] + dot(act_a[...], weight)
    sum_b[...] = near_b[...] + dot(act_b[...], weight)


def gated_kernel(place, near_a, near_b, from_prev, from_next, hidden, gated, sent):
    x = place[1]
    hidden[0] = near_a[...] + from_prev[...].astype(jnp.float32)
    hidden[1] = near_b[...] + from_next[...].astype(jnp.float32)
    gated[...] = act(hidden[...])
    sent[...] = gated[1 - x]


def hidden_grad_kernel(place, hidden, cot_a, cot_b, proj, hg_a, hg_b):
    weight = proj[...]
    hg_a[...] = gelu_grad(hidden[0], dot(cot_a[...], weight)).astype(jnp.bfloat16)
    hg_b[...] = gelu_grad(hidden[1], dot(cot_b[...], weight)).astype(jnp.bfloat16)


def term_kernel(place, rows_a, rows_b, grad_a, grad_b, mine, theirs, product):
    core = place[2]
    sums = t_dot(rows_a[...], grad_a[...]) + t_dot(rows_b[...], grad_b[...])
    product[...] = sums.reshape(product.shape)
    mine[:, 0] = product[:, core]
    theirs[:, 0] = product[:, 1 - core].astype(theirs.dtype)


def turn_kernel(place, rows_a, rows_b, out):
    half = rows_a.shape[0]
    out[:, :half] = rows_a[...].T
    out[:, half:] = rows_b[...].T


def turned_term_kernel(place, turned, grad_a, grad_b, mine, theirs, product):
    core = place[2]
    half = grad_a.shape[0]
    sums = dot(turned[:, :half], grad_a[...]) + dot(turned[:, half:], grad_b[...])
    product[...] = sums.reshape(product.shape)
    mine[:, 0] = product[:, core]
    theirs[:, 0] = product[:, 1 - core].astype(theirs.dtype)


def first_x_kernel(place, mine, got, kept, sent):
    x = place[1]
    kept[...] = mine[x] + got[x].astype(jnp.float32)
    sent[...] = (mine[1 - x] + got[1 - x].astype(jnp.float32)).astype(jnp.bfloat16)


def then_z_kernel(place, mine, got, kept, *sent):
    z = place[0]
    kept[...] = mine[z] + got[z].astype(jnp.float32)
    for k, out in enumerate(sent, 1):
        out[...] = (mine[z ^ k] + got[z ^ k].astype(jnp.float32)).astype(jnp.bfloat16)


def input_grad_kernel(place, hg_next, hg_b, hg_a, hg_prev, w0, w1, w2, in_a, in_b, cot_a, cot_b, kept, sent):
    x = place[1]

    def grad(later, here, earlier, values, cot):
        total = dot_t(later[...], w0[...]) + dot_t(here[...], w1[...]) + dot_t(earlier[...], w2[...])
        wide = values[...].astype(jnp.float32)
        return (cot[...].astype(jnp.float32) + gelu_grad(wide, total)).astype(jnp.bfloat16)

    grad_a = grad(hg_b, hg_a, hg_prev, in_a, cot_a)
    grad_b = grad(hg_next, hg_b, hg_a, in_b, cot_b)

    @pl.when(x == 0)
    def _():
        kept[...] = grad_a
        sent[...] = grad_b

    @pl.when(x != 0)
    def _():
        kept[...] = grad_b
        sent[...] = grad_a


def outputs_kernel(place, gated, got, proj, inputs, outputs):
    x = place[1]
    weight = proj[...]
    for window, rows in ((x, gated[x]), (1 - x, got[...])):
        wide = inputs[window].astype(jnp.float32) + dot_t(rows, weight)
        outputs[window] = wide.astype(jnp.bfloat16)


def paired(inputs, conv_weight, proj_weight, cotangent):
    batch, local_len, chans = inputs.shape
    hid = conv_weight.shape[2]
    devices = lax.axis_size("seq")
    depth = devices // 4
    share = chans // devices
    scale = 1.0 / float(batch * L) ** 0.5
    me, y = lax.axis_index("seq"), lax.axis_index("groups")
    core, x, z = me % 2, (me // 2) % 2, me // 4
    place = jnp.stack([z, x, core, y]).astype(jnp.int32)
    everyone = range(devices)
    bf16, f32 = jnp.bfloat16, jnp.float32
    tile = 256
    steps = chans // tile

    def swap(value, bits):
        return lax.ppermute(value, "seq", [(i, i ^ bits) for i in everyone])

    def up(value):
        return lax.ppermute(value, "seq", [(i, i + 4) for i in everyone if i + 4 in everyone])

    def down(value):
        return lax.ppermute(value, "seq", [(i + 4, i) for i in everyone if i + 4 in everyone])

    def pick(value, index, axis=0):
        return lax.dynamic_index_in_dim(value, index, axis, keepdims=False)

    def ordered(kept, got):
        return jnp.where(x == 0, kept, got), jnp.where(x == 0, got, kept)

    half = share // 2
    shard = jnp.concatenate([conv_weight, proj_weight[None]], axis=0)
    shard = lax.dynamic_slice_in_dim(shard, y * half, half, 1)
    shard_x = swap(shard, 2)
    in_got = swap(after(pick(inputs, 1 - x), shard_x), 2)

    def along_z(piece):
        return jnp.stack([piece] + [swap(piece, 4 * d) for d in range(1, depth)])

    def column(k):
        return jnp.stack([shard[k], shard_x[k]])

    def over_y(column):
        return jnp.stack([column, lax.ppermute(column, "groups", [(0, 1), (1, 0)])])

    def tap_sums(rows_sent, rows_kept, tap):
        return call(
            tap_kernel,
            [((local_len, hid), bf16), ((local_len, hid), f32)],
            place, rows_sent, rows_kept, tap,
            grid=(hid // tile,),
            ins=[RESIDENT] * 2 + [block((chans, tile), 0, 1)],
            out_specs=[block((local_len, tile), 0, 1)] * 2,
        )

    column_0 = along_z(column(0))
    column_2 = along_z(after(column(2), column_0))
    half_0 = over_y(column_0)
    in_a, in_b = ordered(pick(inputs, x), in_got)
    act_a, act_b = act(in_a), act(in_b)
    column_1 = along_z(after(column(1), column_2, half_0))
    half_2 = over_y(after(column_2, half_0))
    w0 = placed(place, half_0, swap(half_0, 1))
    cot_got = swap(after(pick(cotangent, 1 - x), in_got, column_1), 2)
    to_next, near_b = tap_sums(act_b, act_a, w0)
    from_prev = up(to_next)
    w2 = placed(place, half_2, swap(after(half_2, to_next, column_1), 1))
    half_1 = over_y(after(column_1, half_2))
    to_prev, near_a = tap_sums(act_a, act_b, after(w2, to_next))
    from_next = down(to_prev)
    piece_p = after(column(3), column_1, half_2, to_next)
    column_p = [swap(piece_p, 12), swap(piece_p, 8)]
    column_p = jnp.stack([piece_p, swap(after(piece_p, w2), 4)] + column_p[::-1])
    half_p = over_y(after(column_p, half_1, to_prev))
    w1 = placed(place, half_1, swap(half_1, 1))
    near_a, near_b = call(
        own_tap_kernel,
        [((local_len, hid), f32)] * 2,
        place, near_a, near_b, act_a, act_b, w1,
        grid=(hid // tile,),
        ins=[block((local_len, tile), 0, 1)] * 2
        + [RESIDENT] * 2
        + [block((chans, tile), 0, 1)],
        out_specs=[block((local_len, tile), 0, 1)] * 2,
        work=1,
    )
    hidden, gated, gated_sent = call(
        gated_kernel,
        [((2, local_len, hid), f32), ((2, local_len, hid), bf16), ((local_len, hid), bf16)],
        place, near_a, near_b, from_prev, from_next,
        grid=(hid // tile,),
        ins=[block((local_len, tile), 0, 1)] * 4,
        out_specs=[block((2, local_len, tile), 0, 0, 1)] * 2 + [block((local_len, tile), 0, 1)],
    )
    gated_got = swap(gated_sent, 2)

    def turned(rows_a, rows_b):
        cols = 4 * share
        return call(
            turn_kernel,
            [((chans, 2 * local_len), bf16)],
            place, rows_a, rows_b,
            grid=(depth,),
            ins=[block((local_len, cols), 0, 1)] * 2,
            out_specs=[block((cols, 2 * local_len), 1, 0)],
        )[0]

    def term(lhs, grad_a, grad_b, work=1):
        cols = 4 * share
        part = (2, depth, share, hid)
        one = len(lhs) == 1
        mine, theirs = call(
            turned_term_kernel if one else term_kernel,
            [(part, f32), (part, bf16)],
            place, *lhs, grad_a, grad_b,
            grid=(depth,),
            ins=([block((cols, 2 * local_len), 1, 0)] if one else [block((local_len, cols), 0, 1)] * 2) + [RESIDENT] * 2,
            out_specs=[block((2, 1, share, hid), 0, 1, 0, 0)] * 2,
            scratch=[pltpu.VMEM((2, 2, share, hid), f32)],
            work=work,
        )
        return mine, swap(theirs, 1)

    def x_first(mine, got):
        kept, sent = call(
            first_x_kernel,
            [((depth, share, hid), f32), ((depth, share, hid), bf16)],
            place, mine, got,
            grid=(depth,),
            ins=[block((2, 1, share, hid), 0, 1, 0, 0)] * 2,
            out_specs=[block((1, share, hid), 1, 0, 0)] * 2,
        )
        return kept, swap(sent, 2)

    def then_z(kept, got):
        kept, *sent = call(
            then_z_kernel,
            [((share, hid), f32)] + [((share, hid), bf16)] * (depth - 1),
            place, kept, got,
        )
        return [kept] + [swap(value, 4 * k) for k, value in enumerate(sent, 1)]

    def total(parts):
        return sum(part.astype(f32) for part in parts)

    cot_a, cot_b = ordered(pick(cotangent, x), cot_got)
    wp = placed(place, half_p, swap(after(half_p, from_prev, from_next, (near_a, near_b), (cot_a, cot_b)), 1))
    term_p = term((cot_a, cot_b), gated[0], gated[1], 1)
    hg_a, hg_b = call(
        hidden_grad_kernel,
        [((local_len, hid), bf16)] * 2,
        place, hidden, cot_a, cot_b, wp,
        grid=(hid // tile,),
        ins=[block((2, local_len, tile), 0, 0, 1)]
        + [RESIDENT] * 2
        + [block((chans, tile), 0, 1)],
        out_specs=[block((local_len, tile), 0, 1)] * 2,
        work=LONG,
    )
    hg_prev, hg_next = up(hg_b), down(hg_a)

    def input_grads(part, earlier):
        cols = [block((local_len, tile), 0, 1)]
        first = part * steps // 2
        late = pl.BlockSpec((local_len, tile), lambda i: (0, i + first))
        taps = pl.BlockSpec((tile, hid), lambda i: (i + first, 0))
        return call(
            input_grad_kernel,
            [((local_len, chans // 2), bf16)] * 2,
            place, hg_next, hg_b, hg_a, after(hg_prev, earlier), w0, w1, w2, in_a, in_b, cot_a, cot_b,
            grid=(steps // 2,),
            ins=[RESIDENT] * 4 + [taps] * 3 + [late] * 4,
            out_specs=cols * 2,
        )

    grad_p = x_first(after(term_p[0], hg_a, gated_got), term_p[1])
    acted = (turned(act_a, after(act_b, grad_p[0])),)
    term_1 = term(acted, hg_a, after(hg_b, grad_p[0]), 1)

    def finished(got):
        return call(
            outputs_kernel,
            [(inputs.shape, bf16)],
            place, gated, got, wp, inputs,
            grid=(steps,),
            ins=[
                block((2, local_len, hid), 0, 0, 0),
                block((local_len, hid), 0, 0),
                block((tile, hid), 1, 0),
                block((2, local_len, tile), 0, 0, 1),
            ],
            out_specs=[block((2, local_len, tile), 0, 0, 1)],
        )[0]

    term_0 = term(acted, hg_b, after(hg_next, term_1[0], hg_prev), LONG)
    grad_1 = x_first(after(term_1[0], term_0[0], grad_p[1]), term_1[1])
    term_2 = term(acted, hg_prev, after(hg_a, grad_1[0]), 1)
    grad_p = then_z(after(grad_p[0], grad_1[0], term_2[0]), grad_p[1])
    grad_0 = x_first(after(term_0[0], grad_p[0]), term_0[1])
    kept_0, sent_0 = input_grads(0, grad_0[0])
    grad_1 = then_z(after(grad_1[0], sent_0, grad_p), grad_1[1])
    grad_2 = x_first(after(term_2[0], grad_1[0]), term_2[1])
    kept_1, sent_1 = input_grads(1, grad_2[0])
    got_0 = swap(sent_0, 2)
    grad_0 = then_z(after(grad_0[0], sent_1, grad_1), grad_0[1])
    outputs = finished(after(gated_got, got_0))
    grad_2 = then_z(after(grad_2[0], grad_0[0], grad_0, outputs), grad_2[1])
    got_1 = swap(after(sent_1, grad_2[0]), 2)
    input_kept = jnp.concatenate([kept_0, kept_1], axis=1)
    input_got = jnp.concatenate([got_0, got_1], axis=1)
    input_grad = jnp.stack(ordered(input_kept, input_got))
    conv_grad = jnp.stack([total(grad_0), total(grad_1), total(grad_2)], axis=1)
    return (
        outputs,
        input_grad,
        conv_grad * scale,
        total(grad_p) * scale,
    )


def solution(mesh):
    def body(inputs, conv_weight, proj_weight, cotangent):
        devices = lax.axis_size("seq")
        by_pairs = devices == 16 and inputs.shape[0] == 2 and lax.axis_size("groups") == 2
        return (paired if by_pairs else shards)(inputs, conv_weight, proj_weight, cotangent)

    return jax.shard_map(
        body,
        mesh=mesh,
        in_specs=(
            P("groups", "seq", None),
            P(None, "seq", None),
            P("seq", None),
            P("groups", "seq", None),
        ),
        out_specs=(
            P("groups", "seq", None),
            P("groups", "seq", None),
            P(("groups", "seq"), None, None),
            P(("groups", "seq"), None),
        ),
        check_vma=False,
    )
```
